32 devices in a mesh: grp: 2 (over x), row: 16 (over z, y, core).
Axes of the slice: x: 2, y: 2, z: 4, core: 2. Of those that a mesh axis runs over, the one named last changes fastest.
Arguments:
- features: bfloat16 [65536, 128], P(('grp', 'row')), parts along dimension 0, may hold values from -6 to 6
- weight: bfloat16 [128, 256], replicated, may hold values from -0.5 to 0.5
- grad_out: bfloat16 [65536, 256], P(('grp', 'row')), parts along dimension 0, may hold values from -6 to 6
- local_vals: bfloat16 [512, 8, 128, 128], P(('grp', 'row')), parts along dimension 0, may hold values from 0 to 1, as said below
- local_cols: int32 [512, 8], P(('grp', 'row')), parts along dimension 0, may hold values from 0 to 15, all different within a row
- remote_vals: bfloat16 [512, 4, 128, 128], P(('grp', 'row')), parts along dimension 0, may hold values from 0 to 1, as said below
- remote_owner: int32 [512, 4], P(('grp', 'row')), parts along dimension 0, may hold values from 0 to 15, all different within a row; in each aligned block of 16 rows (0 to 15, 16 to 31, ...) at most 8 rows name the same one
- remote_index: int32 [512, 4], P(('grp', 'row')), parts along dimension 0, may hold values from 0 to 15
- remote_flag: int32 [512, 4], P(('grp', 'row')), parts along dimension 0, may hold values 0 or 1
Outputs:
- hidden: bfloat16 [65536, 256], P(('grp', 'row')), parts along dimension 0
- input_grad: bfloat16 [65536, 128], P(('grp', 'row')), parts along dimension 0
- weight_grad: float32 [256, 256], P('grp'), parts along dimension 0
The draws below stay inside these ranges and needn't reach their ends.
There are 2 independent parts, one for each index of `grp`. The reference program is written for one: setup_inputs(seed, part) draws one part's arguments, and reference() takes and returns one part's arrays. A program takes and returns all parts, laid end to end along the dimension named above; an argument that names none is the same for every part. Nothing has to cross between parts.
Inputs may be any that keep to these rules, and one draw needn't show every extreme that they name: `local_vals`: entries are 0 or between 0.1 and 1; a third or more of each tile's entries are nonzero. `remote_vals`: entries are 0 or between 0.1 and 1; a third or more of each tile's entries are nonzero. `local_cols`: the 8 entries of a block row differ. `remote_owner`: the 4 owners of one block row differ; among the tiles of the 16 block rows of one device, no owner is named more than 8 times.
All inputs are finite; a program needn't handle non-finite values. No bound on the sum of `remote_flag` on one device may be relied on, other than what follows from the above.
Results may differ from the reference program's by a relative error of at most 0.0075.
Values may be sent and summed in bfloat16 or wider, within the bound.
A program may use at most 128 MiB of HBM per device.

```python
import math
import jax
import jax.numpy as jnp
import numpy as np
from jax import lax

F = 128
HID = 256
BLK = 128
NB_DEV = 16
LB = 8
TPR = 4
CAP = 8
BLOCKS = 256
NODES = 32768
N_ROW = 16


def tile_values(key, shape):
    key_density, key_value, key_keep = jax.random.split(key, 3)
    density = jax.random.uniform(key_density, shape[:2] + (1, 1), minval=0.35, maxval=0.7)
    values = jnp.exp(jax.random.uniform(key_value, shape, minval=math.log(0.1), maxval=0.0))
    keep = jax.random.uniform(key_keep, shape) < density
    return jnp.where(keep, values, 0.0).astype(jnp.float32).astype(jnp.bfloat16)


def draw_local_vals(key, part):
    key = jax.random.fold_in(key, 11)
    return tile_values(key, (BLOCKS, LB, BLK, BLK))


def draw_remote_vals(key, part):
    key = jax.random.fold_in(key, 23)
    return tile_values(key, (BLOCKS, TPR, BLK, BLK))


def plant(entries, stream_key, least, largest):
    shape = entries.shape
    place = [jax.random.randint(jax.random.fold_in(stream_key, axis), (), 0, shape[axis]) for axis in range(len(shape))]
    entries = entries.at[tuple(place)].set(least)
    longest = shape.index(max(shape))
    place[longest] = (place[longest] + 1) % shape[longest]
    return entries.at[tuple(place)].set(largest)


def block_levels(rng, extent, pieces, low, high):
    loudness = 1.0
    for axis_at, blocks in pieces:
        steps = jax.random.uniform(jax.random.fold_in(jax.random.fold_in(rng, 6), axis_at), (blocks,), jnp.float32, low / len(pieces), high / len(pieces))
        loudness = loudness * jnp.repeat(jnp.exp(steps), extent[axis_at] // blocks).reshape((-1,) + (1,) * (len(extent) - 1 - axis_at))
    return loudness


def different_ones(key, rows, count, top, lift):
    sequence = jax.random.permutation(jax.random.fold_in(key, 1), count)
    favour = sequence
    for power in range(3):
        favour = favour * favour // count
    favour = favour * lift // count
    tickets = jax.random.randint(jax.random.fold_in(key, 2), (rows, count), 0, 4096) + favour
    holders = jax.random.permutation(jax.random.fold_in(key, 3), rows)[jnp.arange(count) % rows]
    tickets = jnp.where(jnp.arange(rows)[:, None] == holders[None, :], 1 << 14, tickets)
    merit = tickets * count + jnp.arange(count)
    return lax.top_k(merit.astype(jnp.int32), top)[1].astype(jnp.int32)


def shared_out(rng, own, number, rows, count, top, most, lean):
    ranking = jax.random.permutation(rng, count)
    heavy_load, usual = portions_of(count, rows * top, most, lean, True), portions_of(count, rows * top, most, lean, False)
    places = jnp.arange(count)

    def named(tallies, rotation):
        used = int((tallies > 0).sum())
        fixed = max(1, used // 4)
        moved = fixed + (places - fixed + rotation * (used - fixed)) % max(1, count - fixed)
        return jnp.zeros((count,), jnp.int32).at[ranking[jnp.where(places < fixed, places, moved)]].set(jnp.asarray(tallies, jnp.int32))

    tallies = jnp.where(number % 4 == 0, named(heavy_load, number // 4), named(usual, number - number // 4 - 1))
    mixed = jax.random.permutation(jax.random.fold_in(own, 3), count)
    giver, sink = mixed[0:count // 2 * 2:2], mixed[1:count // 2 * 2:2]
    slack = jnp.minimum(tallies[giver] - 1, most - tallies[sink]) // 2
    slack = jnp.where((giver == ranking[0]) | (sink == ranking[0]) | (tallies[sink] == 0), 0, jnp.maximum(slack, 0))
    moved = jax.random.randint(jax.random.fold_in(own, 4), (count // 2,), 0, 1 << 20) % (slack + 1)
    tallies = tallies.at[giver].add(-moved).at[sink].add(moved)
    labels = jnp.searchsorted(jnp.cumsum(tallies), jnp.arange(rows * top), side="right").astype(jnp.int32)
    table = labels.reshape(top, rows).T
    table = table[jax.random.permutation(jax.random.fold_in(own, 1), rows)]
    rotation = jax.random.randint(jax.random.fold_in(own, 2), (rows, 1), 0, top)
    return jnp.take_along_axis(table, (jnp.arange(top)[None, :] + rotation) % top, axis=1)


def portions_of(count, total, most, lean, full):
    weights = [(1 << 20) // math.isqrt(standing ** lean) + 1 for standing in range(1, count + 1)]
    largest = most if full else min(most, max(-(-total // count), total * weights[0] // sum(weights)))
    least = 1 if total - largest >= count - 1 else 0
    holding, rest = [largest] + [least] * (count - 1), total - largest - least * (count - 1)
    while rest > 0:
        free = [i for i in range(1, count) if holding[i] < largest] or [i for i in range(1, count) if holding[i] < most]
        pool, left = sum([weights[i] for i in free]), rest
        for i in free:
            extra = min(most - holding[i], max(1, left * weights[i] // pool), rest)
            holding[i] = holding[i] + extra
            rest = rest - extra
    return np.array(holding)


def noise(own_key, extent, width, most, cuts=(), kind=jnp.bfloat16):
    loudness = block_levels(own_key, extent, cuts, -0.22, 0.18) if cuts else 1.0
    result = jax.random.normal(own_key, extent, jnp.float32) * width * loudness
    return jnp.minimum(jnp.maximum(result, -most), most).astype(kind)


def setup_inputs(seed: int = 0, part: int = 0) -> dict:
    streams_of = jax.random.split(jax.random.key(seed), 10)
    own_keys = jax.random.split(jax.random.fold_in(streams_of[9], part), 10)
    features = noise(own_keys[0], (NODES, F), 1.0, 6.0, ((0, 16),))
    weight = noise(streams_of[1], (F, HID), F ** -0.5, 0.5)
    grad_out = noise(own_keys[2], (NODES, HID), 1.0, 6.0, ((0, 16),))
    local_vals = draw_local_vals(jax.random.fold_in(jax.random.fold_in(streams_of[9], part), 71), part)
    local_cols = different_ones(own_keys[4], BLOCKS, NB_DEV, LB, 0)
    remote_vals = draw_remote_vals(jax.random.fold_in(jax.random.fold_in(streams_of[9], part), 71), part)
    remote_owner_keys = jax.random.split(jax.random.fold_in(own_keys[6], 1), BLOCKS // NB_DEV)
    remote_owner_turns = jax.random.permutation(jax.random.fold_in(own_keys[6], 3), BLOCKS // NB_DEV)
    remote_owner = jax.vmap(lambda own, number: shared_out(jax.random.fold_in(own_keys[6], 2), own, number, NB_DEV, N_ROW, TPR, CAP, 2))(remote_owner_keys, remote_owner_turns).reshape((BLOCKS, TPR))
    remote_index = plant(jax.random.randint(own_keys[7], (BLOCKS, TPR), 0, NB_DEV), jax.random.fold_in(own_keys[7], 1), 0, NB_DEV - 1).astype(jnp.int32)
    remote_flag = plant((jax.random.randint(own_keys[8], (BLOCKS, TPR), 0, 4) < 3).astype(jnp.int32), jax.random.fold_in(own_keys[8], 1), 0, 1)
    return {"features": features, "weight": weight, "grad_out": grad_out, "local_vals": local_vals, "local_cols": local_cols, "remote_vals": remote_vals, "remote_owner": remote_owner, "remote_index": remote_index, "remote_flag": remote_flag}


def reference(features, weight, grad_out, local_vals, local_cols, remote_vals, remote_owner, remote_index, remote_flag):
    xblocks = features.reshape(BLOCKS, BLK, F)
    base = jnp.arange(BLOCKS, dtype=jnp.int32) // NB_DEV * NB_DEV
    cols_all = jnp.concatenate([base[:, None] + local_cols, remote_owner * NB_DEV + remote_index], axis=1).astype(jnp.int32)
    masked = remote_vals * remote_flag[:, :, None, None].astype(jnp.bfloat16)
    vals_all = jnp.concatenate([local_vals, masked], axis=1)

    def one_row(item):
        vals, cols = item
        blocks = xblocks[cols]
        return jnp.einsum('tij,tjf->if', vals.astype(jnp.float32), blocks.astype(jnp.float32))
    summed = lax.map(one_row, (vals_all, cols_all))
    agg = (xblocks.astype(jnp.float32) + summed).reshape(NODES, F).astype(jnp.bfloat16)
    degree = lax.optimization_barrier(jnp.sum(vals_all, axis=(1, 3), dtype=jnp.float32)).reshape(NODES)
    norm = lax.rsqrt(1.0 + degree)
    z = norm[:, None] * jnp.dot(agg, weight, preferred_element_type=jnp.float32)
    out, pull = jax.vjp(jax.nn.gelu, z)
    hidden = out.astype(jnp.bfloat16)
    grad_z = pull(grad_out.astype(jnp.float32))[0]
    gs = (norm[:, None] * grad_z).astype(jnp.bfloat16)
    weight_grad = lax.dot_general(agg, gs, (((0,), (0,)), ((), ())), preferred_element_type=jnp.float32) * (1.0 / math.sqrt(NODES))
    dagg = lax.dot_general(gs, weight, (((1,), (1,)), ((), ())), preferred_element_type=jnp.float32).astype(jnp.bfloat16)
    dblocks = dagg.reshape(BLOCKS, BLK, F)

    def add_row(total, item):
        vals, cols, grads = item
        terms = jnp.einsum('tij,if->tjf', vals.astype(jnp.float32), grads.astype(jnp.float32))
        rounded = lax.optimization_barrier(terms[LB:].astype(jnp.bfloat16)).astype(jnp.float32)
        terms = jnp.concatenate([terms[:LB], rounded], axis=0)
        return (total.at[cols].add(terms), None)
    start = jnp.zeros((BLOCKS, BLK, F), jnp.float32)
    back, _ = lax.scan(add_row, start, (vals_all, cols_all, dblocks))
    input_grad = (dblocks.astype(jnp.float32) + back).reshape(NODES, F).astype(jnp.bfloat16)
    return (hidden, input_grad, weight_grad)
```

```python
import functools
import math

import jax
import jax.numpy as jnp
from jax import lax
from jax.experimental import pallas as pl
from jax.experimental.pallas import tpu as pltpu
from jax.sharding import PartitionSpec as P


def slotted(
    features,
    weight,
    grad_out,
    local_vals,
    local_cols,
    remote_vals,
    remote_owner,
    remote_index,
    remote_flag,
):
    block_size = local_vals.shape[2]
    blocks_dev = local_vals.shape[0]
    tiles_row = remote_vals.shape[1]
    feat = features.shape[1]
    row_count = lax.axis_size("row")
    slot_cap = max(2, 2 * blocks_dev * tiles_row // row_count)
    tile_count = blocks_dev * tiles_row
    node_count = blocks_dev * block_size
    xblocks = features.reshape(blocks_dev, block_size, feat)
    owners = remote_owner.reshape(-1)
    owner_hot = (owners[:, None] == jnp.arange(row_count, dtype=jnp.int32)[None, :]).astype(
        jnp.int32
    )
    ranks = jnp.sum((jnp.cumsum(owner_hot, axis=0) - owner_hot) * owner_hot, axis=1)
    slot_flat = owners * slot_cap + ranks
    request = (
        jnp.zeros((row_count * slot_cap,), jnp.int32).at[slot_flat].set(remote_index.reshape(-1))
    )
    request = request.reshape(row_count, slot_cap)
    masked = remote_vals * remote_flag[:, :, None, None].astype(jnp.bfloat16)
    tiles_flat = masked.reshape(tile_count, block_size, block_size)
    piece = lax.all_to_all(request, "row", split_axis=0, concat_axis=0, tiled=True)
    found = xblocks[piece]
    returned = lax.all_to_all(found, "row", split_axis=0, concat_axis=0, tiled=True)
    remote_x = returned.reshape(row_count * slot_cap, block_size, feat)[slot_flat]
    remote_sum = jnp.einsum(
        "tij,tjf->tif", tiles_flat, remote_x, preferred_element_type=jnp.float32
    )
    remote_sum = jnp.sum(remote_sum.reshape(blocks_dev, tiles_row, block_size, feat), axis=1)
    local_x = xblocks[local_cols]
    local_sum = jnp.einsum(
        "rlij,rljf->rif", local_vals, local_x, preferred_element_type=jnp.float32
    )
    agg = (
        (xblocks.astype(jnp.float32) + local_sum + remote_sum)
        .reshape(node_count, feat)
        .astype(jnp.bfloat16)
    )
    degree = jnp.sum(local_vals, axis=(1, 3), dtype=jnp.float32) + jnp.sum(
        masked, axis=(1, 3), dtype=jnp.float32
    )
    norm = lax.rsqrt(1.0 + degree.reshape(node_count))
    z_value = norm[:, None] * jnp.dot(agg, weight, preferred_element_type=jnp.float32)
    activated, pull = jax.vjp(jax.nn.gelu, z_value)
    hidden = activated.astype(jnp.bfloat16)
    grad_z = pull(grad_out.astype(jnp.float32))[0]
    scaled_grad = (norm[:, None] * grad_z).astype(jnp.bfloat16)
    weight_term = lax.dot_general(
        agg, scaled_grad, (((0,), (0,)), ((), ())), preferred_element_type=jnp.float32
    )
    total_nodes = node_count * row_count
    weight_grad = lax.psum(weight_term, "row") * (1.0 / math.sqrt(total_nodes))
    dagg = lax.dot_general(
        scaled_grad, weight, (((1,), (1,)), ((), ())), preferred_element_type=jnp.float32
    ).astype(jnp.bfloat16)
    dblocks = dagg.reshape(blocks_dev, block_size, feat)
    local_hot = (
        local_cols[:, :, None] == jnp.arange(blocks_dev, dtype=jnp.int32)[None, None, :]
    ).astype(jnp.float32)
    local_terms = jnp.einsum(
        "rlij,rif->rljf", local_vals, dblocks, preferred_element_type=jnp.float32
    )
    local_back = jnp.einsum("rlk,rljf->kjf", local_hot, local_terms)
    asked_hot = (
        piece[:, :, None] == jnp.arange(blocks_dev, dtype=jnp.int32)[None, None, :]
    ).astype(jnp.bfloat16)
    sender_terms = jnp.einsum(
        "rtij,rif->rtjf", masked, dblocks, preferred_element_type=jnp.float32
    ).astype(jnp.bfloat16)
    part_send = (
        jnp.zeros((row_count * slot_cap, block_size, feat), jnp.bfloat16)
        .at[slot_flat]
        .set(sender_terms.reshape(tile_count, block_size, feat))
    )
    received = lax.all_to_all(
        part_send.reshape(row_count, slot_cap, block_size, feat),
        "row",
        split_axis=0,
        concat_axis=0,
        tiled=True,
    )
    remote_back = jnp.einsum(
        "sck,scjf->kjf", asked_hot, received, preferred_element_type=jnp.float32
    )
    input_grad = (
        (dblocks.astype(jnp.float32) + local_back + remote_back)
        .reshape(node_count, feat)
        .astype(jnp.bfloat16)
    )
    return (hidden, input_grad, weight_grad)


MESH = pl.DeviceIdType.MESH
RIGHT, LEFT, ACROSS, SIBLING = 0, 1, 2, 3
PIECES = 4


def place():
    me = lax.axis_index("row")
    core = lax.rem(me, 2)
    yy = lax.rem(lax.div(me, 2), 2)
    zz = lax.div(me, 4)
    return me, core, yy, zz, me + 1 - 2 * core, me + 2 - 4 * yy


def signal(barrier, device):
    pl.semaphore_signal(barrier, inc=1, device_id={"row": device}, device_id_type=MESH)


def gather_kernel(zs, x_ref, out_ref, own_sem, send_sem, recv_sem):
    me, core, yy, zz, sib, ynb = place()
    rows = x_ref.shape[0] // PIECES
    has_left, has_right = zz > 0, zz < zs - 1

    barrier = pltpu.get_barrier_semaphore()
    signal(barrier, sib)
    signal(barrier, ynb)
    pl.when(has_left)(lambda: signal(barrier, me - 4))
    pl.when(has_right)(lambda: signal(barrier, me + 4))
    pl.semaphore_wait(barrier, 2 + has_left.astype(jnp.int32) + has_right.astype(jnp.int32))

    own = pltpu.make_async_copy(x_ref, out_ref.at[me], own_sem)
    own.start()

    def copy(kind, shard, j, device, mine=False):
        zt = lax.div(shard, 4)
        slot = zt if kind != SIBLING else zt + zs * lax.rem(lax.div(shard, 2), 2)
        cut = pl.ds(pl.multiple_of(j * rows, rows), rows)
        there = out_ref.at[shard, cut]
        return pltpu.make_async_remote_copy(
            src_ref=x_ref.at[cut] if mine else there,
            dst_ref=there,
            send_sem=send_sem.at[kind * zs + slot, j],
            recv_sem=recv_sem.at[shard, j],
            device_id={"row": device},
            device_id_type=MESH,
        )

    def each(body):
        lax.fori_loop(0, PIECES, lambda j, c: (body(j), c)[1], 0)

    def own_sends(act):
        def body(j):
            pl.when(has_right)(lambda: act(copy(RIGHT, me, j, me + 4, True)))
            pl.when(has_left)(lambda: act(copy(LEFT, me, j, me - 4, True)))
            act(copy(ACROSS, me, j, ynb, True))
            act(copy(SIBLING, me, j, sib, True))

        each(body)

    def along(act, wait):
        for k in range(1, zs):
            for sign in (-1, 1):
                shard = me + sign * 4 * k
                onward = has_right if sign < 0 else has_left
                kind = RIGHT if sign < 0 else LEFT

                def body(j, shard=shard, onward=onward, kind=kind, sign=sign):
                    if wait:
                        copy(SIBLING, shard, j, sib).wait_recv()
                    pl.when(onward)(lambda: act(copy(kind, shard, j, me - sign * 4)))
                    act(copy(ACROSS, shard, j, ynb))
                    act(copy(SIBLING, shard, j, sib))

                pl.when(zz >= k if sign < 0 else zz + k < zs)(functools.partial(each, body))

    def across(act, wait):
        for k in range(zs):
            for sign in (-1, 1):
                if k == 0 and sign == 1:
                    continue
                shard = ynb + sign * 4 * k

                def body(j, shard=shard):
                    if wait:
                        copy(SIBLING, shard, j, sib).wait_recv()
                    act(copy(SIBLING, shard, j, sib))

                pl.when(zz >= k if sign < 0 else zz + k < zs)(functools.partial(each, body))

    start = lambda c: c.start()
    finish = lambda c: c.wait_send()
    own_sends(start)
    along(start, True)
    across(start, True)
    for q in range(2 * zs):
        shard = 2 * q + 1 - core
        each(lambda j, shard=shard: copy(SIBLING, shard, j, sib).wait_recv())
    own.wait()
    own_sends(finish)
    along(finish, False)
    across(finish, False)


def gather(x, row_count):
    zs = row_count // 4
    return pl.pallas_call(
        functools.partial(gather_kernel, zs),
        out_shape=jax.ShapeDtypeStruct((row_count,) + x.shape, x.dtype),
        in_specs=[pl.BlockSpec(memory_space=pl.ANY)],
        out_specs=pl.BlockSpec(memory_space=pl.ANY),
        scratch_shapes=[
            pltpu.SemaphoreType.DMA,
            pltpu.SemaphoreType.DMA((5 * zs, PIECES)),
            pltpu.SemaphoreType.DMA((row_count, PIECES)),
        ],
        compiler_params=pltpu.CompilerParams(collective_id=0, has_side_effects=True),
        name="gather_features",
    )(x)


def layer_kernel(
    tiles_row,
    lcol,
    rcol,
    flag,
    x_ref,
    *refs,
):
    far = refs[:tiles_row]
    weight_ref, grad_ref, lv_ref, rv_ref, hidden_ref, part_ref, base_ref, wg_ref = refs[tiles_row:]
    r = pl.program_id(0)
    lb = lv_ref.shape[1]
    block, feat = lv_ref.shape[2], x_ref.shape[2]
    f32, bf16 = jnp.float32, jnp.bfloat16

    @pl.when(r == 0)
    def _():
        base_ref[...] = jnp.zeros_like(base_ref)
        wg_ref[...] = jnp.zeros_like(wg_ref)

        def clear(i, c):
            part_ref[i] = jnp.zeros(part_ref.shape[1:], bf16)
            return c

        lax.fori_loop(0, part_ref.shape[0], clear, 0)

    ones = jnp.ones((block, feat), bf16)
    flags = [flag[r * tiles_row + t].astype(f32) for t in range(tiles_row)]
    tiles = [lv_ref[0, l] for l in range(lb)] + [rv_ref[0, t] for t in range(tiles_row)]
    blocks = [jnp.concatenate([x_ref[lcol[r * lb + l]], ones], axis=1) for l in range(lb)]
    for t in range(tiles_row):
        seen = jnp.concatenate([far[t][0], ones], axis=1)
        blocks.append((seen.astype(f32) * flags[t]).astype(bf16))
    total = jnp.dot(
        jnp.concatenate(tiles, axis=1),
        jnp.concatenate(blocks, axis=0),
        preferred_element_type=f32,
    )
    agg = (x_ref[r].astype(f32) + total[:, :feat]).astype(bf16)
    norm = lax.rsqrt(1.0 + total[:, feat:])
    hid = weight_ref.shape[1]
    norm = jnp.concatenate([norm] * (hid // feat), axis=1)
    v = norm * jnp.dot(agg, weight_ref[...], preferred_element_type=f32)
    scale = math.sqrt(2.0 / math.pi)
    square = v * v
    t = jnp.tanh(scale * (v + 0.044715 * (square * v)))
    half = 0.5 * (1.0 + t)
    hidden_ref[...] = (v * half).astype(bf16)
    slope = half + (0.5 * scale) * v * (1.0 - t * t) * (1.0 + (3 * 0.044715) * square)
    gs = (norm * (grad_ref[...].astype(f32) * slope)).astype(bf16)
    wg_ref[...] += lax.dot_general(agg, gs, (((0,), (0,)), ((), ())), preferred_element_type=f32)
    dagg = lax.dot_general(
        weight_ref[...], gs, (((1,), (1,)), ((), ())), preferred_element_type=f32
    ).astype(bf16)
    base_ref[r] += dagg.astype(f32)
    terms = jnp.dot(dagg, jnp.concatenate(tiles, axis=1), preferred_element_type=f32)
    for l in range(lb):
        base_ref[lcol[r * lb + l]] += terms[:, l * block : (l + 1) * block]
    for t in range(tiles_row):
        at = rcol[r * tiles_row + t]
        term = terms[:, (lb + t) * block : (lb + t + 1) * block] * flags[t]
        part_ref[at] = (part_ref[at].astype(f32) + term).astype(bf16)


def layer(x, seen, weight, grad_out, local_vals, remote_vals, lcol, rcol, flag):
    blocks_dev, lb, block, _ = local_vals.shape
    tiles_row = remote_vals.shape[1]
    feat, hid = weight.shape
    whole = lambda *shape: pl.BlockSpec(shape, lambda r, *_: (0,) * len(shape))
    far = [
        pl.BlockSpec((1, block, feat), lambda r, lc, rc, fl, t=t: (rc[r * tiles_row + t], 0, 0))
        for t in range(tiles_row)
    ]
    return pl.pallas_call(
        functools.partial(layer_kernel, tiles_row),
        grid_spec=pltpu.PrefetchScalarGridSpec(
            num_scalar_prefetch=3,
            grid=(blocks_dev,),
            in_specs=[whole(blocks_dev, block, feat)]
            + far
            + [
                whole(feat, hid),
                pl.BlockSpec((block, hid), lambda r, *_: (r, 0)),
                pl.BlockSpec((1, lb, block, block), lambda r, *_: (r, 0, 0, 0)),
                pl.BlockSpec((1, tiles_row, block, block), lambda r, *_: (r, 0, 0, 0)),
            ],
            out_specs=[
                pl.BlockSpec((block, hid), lambda r, *_: (r, 0)),
                whole(seen.shape[0], feat, block),
                whole(blocks_dev, feat, block),
                whole(feat, hid),
            ],
        ),
        out_shape=[
            jax.ShapeDtypeStruct((blocks_dev * block, hid), jnp.bfloat16),
            jax.ShapeDtypeStruct((seen.shape[0], feat, block), jnp.bfloat16),
            jax.ShapeDtypeStruct((blocks_dev, feat, block), jnp.float32),
            jax.ShapeDtypeStruct((feat, hid), jnp.float32),
        ],
        compiler_params=pltpu.CompilerParams(
            dimension_semantics=("arbitrary",), vmem_limit_bytes=48 << 20
        ),
        name="layer",
    )(lcol, rcol, flag, x, *([seen] * tiles_row), weight, grad_out, local_vals, remote_vals)


def scatter_kernel(
    zs,
    part_ref,
    base_ref,
    w_ref,
    out_ref,
    wout_ref,
    mine,
    from_core,
    from_y,
    from_z,
    held,
    base_sum,
    w_in,
    w_sum,
    load_sem,
    send_sem,
    core_sem,
    y_sem,
    z_sem,
    w_send,
    w_recv,
):
    me, core, yy, zz, sib, ynb = place()
    rows = part_ref.shape[1] // PIECES
    has_left, has_right = zz > 0, zz < zs - 1
    f32, bf16 = jnp.float32, jnp.bfloat16
    near = me + 4 * (1 - 2 * lax.rem(zz, 2))
    apart = me + 8 * (1 - 2 * lax.div(zz, 2))

    def load(zt, yt):
        q = yt * zs + zt
        return pltpu.make_async_copy(
            part_ref.at[zt * 4 + yt * 2 + core], mine.at[q], load_sem.at[q]
        )

    for yt in range(2):
        for zt in range(zs):
            load(zt, yt).start()

    barrier = pltpu.get_barrier_semaphore()
    signal(barrier, sib)
    signal(barrier, ynb)
    signal(barrier, apart)
    pl.when(has_left)(lambda: signal(barrier, me - 4))
    pl.when(has_right)(lambda: signal(barrier, me + 4))
    pl.semaphore_wait(barrier, 3 + has_left.astype(jnp.int32) + has_right.astype(jnp.int32))

    def each(body):
        lax.fori_loop(0, PIECES, lambda j, c: (body(j), c)[1], 0)

    def cut(j):
        return pl.ds(pl.multiple_of(j * rows, rows), rows)

    def remote(src, dst, send, recv, device):
        return pltpu.make_async_remote_copy(
            src_ref=src,
            dst_ref=dst,
            send_sem=send,
            recv_sem=recv,
            device_id={"row": device},
            device_id_type=MESH,
        )

    wrows = w_ref.shape[0] // 2
    kept = pl.ds(pl.multiple_of(core * wrows, wrows), wrows)
    given = pl.ds(pl.multiple_of((1 - core) * wrows, wrows), wrows)
    w_steps = [
        remote(w_ref.at[given], w_in.at[0], w_send.at[0], w_recv.at[0], sib),
        remote(w_sum.at[0], w_in.at[1], w_send.at[1], w_recv.at[1], ynb),
        remote(w_sum.at[1], w_in.at[2], w_send.at[2], w_recv.at[2], near),
        remote(w_sum.at[2], w_in.at[3], w_send.at[3], w_recv.at[3], apart),
    ]
    w_last = remote(wout_ref.at[kept], wout_ref.at[kept], w_send.at[4], w_recv.at[4], sib)
    w_back = remote(wout_ref.at[given], wout_ref.at[given], w_send.at[4], w_recv.at[4], sib)

    def w_go(step):
        w_steps[step].wait_recv()
        held_so_far = w_ref[kept] if step == 0 else w_sum[step - 1]
        total = held_so_far + w_in[step]
        if step < 3:
            w_sum[step] = total
            w_steps[step + 1].start()
        else:
            wout_ref[kept] = total
            w_last.start()

    w_steps[0].start()

    def valid(sign, d):
        return zz >= d if sign < 0 else zz + d < zs

    def order(least):
        for d in range(zs - 1, least - 1, -1):
            for sign in (1, -1) if d else (1,):
                yield d, sign

    def to_core(zt, yt, j):
        return remote(
            part_ref.at[zt * 4 + yt * 2 + 1 - core, cut(j)],
            from_core.at[yt * zs + zt, cut(j)],
            send_sem.at[yt * zs + zt, j],
            core_sem.at[yt * zs + zt, j],
            sib,
        )

    def to_y(zt, j):
        return remote(
            held.at[(1 - yy) * zs + zt, cut(j)],
            from_y.at[zt, cut(j)],
            send_sem.at[2 * zs + zt, j],
            y_sem.at[zt, j],
            ynb,
        )

    def to_z(zt, way, j, device):
        return remote(
            held.at[yy * zs + zt, cut(j)],
            from_z.at[way, zt, cut(j)],
            send_sem.at[3 * zs + zt, j],
            z_sem.at[way, zt, j],
            device,
        )

    for yt in (1 - yy, yy):
        for d, sign in order(0):
            zt = zz + sign * d
            pl.when(valid(sign, d))(
                functools.partial(each, lambda j, zt=zt, yt=yt: to_core(zt, yt, j).start())
            )

    w_go(0)
    step = 1
    for d, sign in order(0):
        zt = zz + sign * d

        @pl.when(valid(sign, d))
        def _(zt=zt):
            q = (1 - yy) * zs + zt
            load(zt, 1 - yy).wait()

            def body(j):
                to_core(zt, 1 - yy, j).wait_recv()
                total = mine[q, cut(j)].astype(f32) + from_core[q, cut(j)].astype(f32)
                held[q, cut(j)] = total.astype(bf16)
                to_y(zt, j).start()

            each(body)

    def summed(zt, j):
        q = yy * zs + zt
        to_core(zt, yy, j).wait_recv()
        to_y(zt, j).wait_recv()
        total = mine[q, cut(j)].astype(f32) + from_core[q, cut(j)].astype(f32)
        return total + from_y[zt, cut(j)].astype(f32)

    w_go(1)
    step = 2
    for d, sign in order(1):
        zt = zz + sign * d
        way = 0 if sign > 0 else 1
        behind = has_left if sign > 0 else has_right

        @pl.when(valid(sign, d))
        def _(zt=zt, way=way, behind=behind, sign=sign):
            load(zt, yy).wait()

            def body(j):
                total = summed(zt, j)
                q = yy * zs + zt

                @pl.when(behind)
                def _():
                    to_z(zt, way, j, me + sign * 4).wait_recv()
                    held[q, cut(j)] = (total + from_z[way, zt, cut(j)].astype(f32)).astype(bf16)

                @pl.when(jnp.logical_not(behind))
                def _():
                    held[q, cut(j)] = total.astype(bf16)

                to_z(zt, way, j, me + sign * 4).start()

            each(body)

        if sign < 0 and step < 4:
            w_go(step)
            step += 1

    load(zz, yy).wait()

    def last(j):
        base_sum[cut(j)] = base_ref[cut(j)] + summed(zz, j)

        @pl.when(has_left)
        def _():
            to_z(zz, 0, j, sib).wait_recv()
            base_sum[cut(j)] += from_z[0, zz, cut(j)].astype(f32)

        @pl.when(has_right)
        def _():
            to_z(zz, 1, j, sib).wait_recv()
            base_sum[cut(j)] += from_z[1, zz, cut(j)].astype(f32)

        out_ref[cut(j)] = base_sum[cut(j)].astype(bf16)

    each(last)

    w_back.wait_recv()
    for c in w_steps:
        c.wait_send()
    w_last.wait_send()
    for zt in range(zs):
        each(lambda j, zt=zt: to_core(zt, 0, j).wait_send())
        each(lambda j, zt=zt: to_core(zt, 1, j).wait_send())
        each(lambda j, zt=zt: to_y(zt, j).wait_send())
        pl.when(zz != zt)(
            functools.partial(each, lambda j, zt=zt: to_z(zt, 0, j, sib).wait_send())
        )


def scatter(part, base, wterm, row_count):
    zs = row_count // 4
    nodes, feat = base.shape
    vmem = pl.BlockSpec(memory_space=pltpu.VMEM)
    dma = pltpu.SemaphoreType.DMA
    shard = lambda *lead: pltpu.VMEM(lead + (nodes, feat), jnp.bfloat16)
    wshape = (wterm.shape[0] // 2, wterm.shape[1])
    return pl.pallas_call(
        functools.partial(scatter_kernel, zs),
        out_shape=[
            jax.ShapeDtypeStruct((nodes, feat), jnp.bfloat16),
            jax.ShapeDtypeStruct(wterm.shape, jnp.float32),
        ],
        in_specs=[pl.BlockSpec(memory_space=pl.ANY), vmem, vmem],
        out_specs=[vmem, vmem],
        scratch_shapes=[
            shard(2 * zs),
            shard(2 * zs),
            shard(zs),
            shard(2, zs),
            shard(2 * zs),
            pltpu.VMEM((nodes, feat), jnp.float32),
            pltpu.VMEM((4,) + wshape, jnp.float32),
            pltpu.VMEM((3,) + wshape, jnp.float32),
            dma((2 * zs,)),
            dma((4 * zs, PIECES)),
            dma((2 * zs, PIECES)),
            dma((zs, PIECES)),
            dma((2, zs, PIECES)),
            dma((5,)),
            dma((5,)),
        ],
        compiler_params=pltpu.CompilerParams(
            collective_id=1, has_side_effects=True, vmem_limit_bytes=48 << 20
        ),
        name="scatter_gradient",
    )(part, base, wterm)


def planned(
    features,
    weight,
    grad_out,
    local_vals,
    local_cols,
    remote_vals,
    remote_owner,
    remote_index,
    remote_flag,
):
    blocks_dev, _, block, _ = local_vals.shape
    nodes, feat = features.shape
    row_count = lax.axis_size("row")
    seen = gather(features, row_count).reshape(row_count * blocks_dev, block, feat)
    rcol = (remote_owner * blocks_dev + remote_index).reshape(-1)
    hidden, part, base, wterm = layer(
        features.reshape(blocks_dev, block, feat),
        seen,
        weight,
        grad_out,
        local_vals,
        remote_vals,
        local_cols.reshape(-1),
        rcol,
        remote_flag.reshape(-1),
    )
    back, wsum = scatter(
        part.reshape(row_count, nodes, feat), base.reshape(nodes, feat), wterm, row_count
    )
    input_grad = jnp.swapaxes(back.reshape(blocks_dev, feat, block), 1, 2).reshape(nodes, feat)
    weight_grad = wsum * (1.0 / math.sqrt(nodes * row_count))
    return hidden, input_grad, weight_grad


def solution(mesh):
    return jax.shard_map(
        planned if mesh.shape["row"] == 16 else slotted,
        mesh=mesh,
        in_specs=(
            P(("grp", "row"), None),
            P(),
            P(("grp", "row"), None),
            P(("grp", "row"), None, None, None),
            P(("grp", "row"), None),
            P(("grp", "row"), None, None, None),
            P(("grp", "row"), None),
            P(("grp", "row"), None),
            P(("grp", "row"), None),
        ),
        out_specs=(P(("grp", "row"), None), P(("grp", "row"), None), P("grp", None)),
        check_vma=False,
    )
```

```python
import functools
import math

import jax
import jax.numpy as jnp
from jax import lax
from jax.experimental import pallas as pl
from jax.experimental.pallas import tpu as pltpu
from jax.sharding import PartitionSpec as P


def slotted(
    features,
    weight,
    grad_out,
    local_vals,
    local_cols,
    remote_vals,
    remote_owner,
    remote_index,
    remote_flag,
):
    block_size = local_vals.shape[2]
    blocks_dev = local_vals.shape[0]
    tiles_row = remote_vals.shape[1]
    feat = features.shape[1]
    row_count = lax.axis_size("row")
    slot_cap = max(2, 2 * blocks_dev * tiles_row // row_count)
    tile_count = blocks_dev * tiles_row
    node_count = blocks_dev * block_size
    xblocks = features.reshape(blocks_dev, block_size, feat)
    owners = remote_owner.reshape(-1)
    owner_hot = (owners[:, None] == jnp.arange(row_count, dtype=jnp.int32)[None, :]).astype(
        jnp.int32
    )
    ranks = jnp.sum((jnp.cumsum(owner_hot, axis=0) - owner_hot) * owner_hot, axis=1)
    slot_flat = owners * slot_cap + ranks
    request = (
        jnp.zeros((row_count * slot_cap,), jnp.int32).at[slot_flat].set(remote_index.reshape(-1))
    )
    request = request.reshape(row_count, slot_cap)
    masked = remote_vals * remote_flag[:, :, None, None].astype(jnp.bfloat16)
    tiles_flat = masked.reshape(tile_count, block_size, block_size)
    piece = lax.all_to_all(request, "row", split_axis=0, concat_axis=0, tiled=True)
    found = xblocks[piece]
    returned = lax.all_to_all(found, "row", split_axis=0, concat_axis=0, tiled=True)
    remote_x = returned.reshape(row_count * slot_cap, block_size, feat)[slot_flat]
    remote_sum = jnp.einsum(
        "tij,tjf->tif", tiles_flat, remote_x, preferred_element_type=jnp.float32
    )
    remote_sum = jnp.sum(remote_sum.reshape(blocks_dev, tiles_row, block_size, feat), axis=1)
    local_x = xblocks[local_cols]
    local_sum = jnp.einsum(
        "rlij,rljf->rif", local_vals, local_x, preferred_element_type=jnp.float32
    )
    agg = (
        (xblocks.astype(jnp.float32) + local_sum + remote_sum)
        .reshape(node_count, feat)
        .astype(jnp.bfloat16)
    )
    degree = jnp.sum(local_vals, axis=(1, 3), dtype=jnp.float32) + jnp.sum(
        masked, axis=(1, 3), dtype=jnp.float32
    )
    norm = lax.rsqrt(1.0 + degree.reshape(node_count))
    z_value = norm[:, None] * jnp.dot(agg, weight, preferred_element_type=jnp.float32)
    activated, pull = jax.vjp(jax.nn.gelu, z_value)
    hidden = activated.astype(jnp.bfloat16)
    grad_z = pull(grad_out.astype(jnp.float32))[0]
    scaled_grad = (norm[:, None] * grad_z).astype(jnp.bfloat16)
    weight_term = lax.dot_general(
        agg, scaled_grad, (((0,), (0,)), ((), ())), preferred_element_type=jnp.float32
    )
    total_nodes = node_count * row_count
    weight_grad = lax.psum(weight_term, "row") * (1.0 / math.sqrt(total_nodes))
    dagg = lax.dot_general(
        scaled_grad, weight, (((1,), (1,)), ((), ())), preferred_element_type=jnp.float32
    ).astype(jnp.bfloat16)
    dblocks = dagg.reshape(blocks_dev, block_size, feat)
    local_hot = (
        local_cols[:, :, None] == jnp.arange(blocks_dev, dtype=jnp.int32)[None, None, :]
    ).astype(jnp.float32)
    local_terms = jnp.einsum(
        "rlij,rif->rljf", local_vals, dblocks, preferred_element_type=jnp.float32
    )
    local_back = jnp.einsum("rlk,rljf->kjf", local_hot, local_terms)
    asked_hot = (
        piece[:, :, None] == jnp.arange(blocks_dev, dtype=jnp.int32)[None, None, :]
    ).astype(jnp.bfloat16)
    sender_terms = jnp.einsum(
        "rtij,rif->rtjf", masked, dblocks, preferred_element_type=jnp.float32
    ).astype(jnp.bfloat16)
    part_send = (
        jnp.zeros((row_count * slot_cap, block_size, feat), jnp.bfloat16)
        .at[slot_flat]
        .set(sender_terms.reshape(tile_count, block_size, feat))
    )
    received = lax.all_to_all(
        part_send.reshape(row_count, slot_cap, block_size, feat),
        "row",
        split_axis=0,
        concat_axis=0,
        tiled=True,
    )
    remote_back = jnp.einsum(
        "sck,scjf->kjf", asked_hot, received, preferred_element_type=jnp.float32
    )
    input_grad = (
        (dblocks.astype(jnp.float32) + local_back + remote_back)
        .reshape(node_count, feat)
        .astype(jnp.bfloat16)
    )
    return (hidden, input_grad, weight_grad)


MESH = pl.DeviceIdType.MESH
RIGHT, LEFT, ACROSS, SIBLING = 0, 1, 2, 3
PIECES = 4


def place():
    me = lax.axis_index("row")
    core = lax.rem(me, 2)
    yy = lax.rem(lax.div(me, 2), 2)
    zz = lax.div(me, 4)
    return me, core, yy, zz, me + 1 - 2 * core, me + 2 - 4 * yy


def signal(barrier, device):
    pl.semaphore_signal(barrier, inc=1, device_id={"row": device}, device_id_type=MESH)


def gather_kernel(zs, x_ref, out_ref, own_sem, send_sem, recv_sem):
    me, core, yy, zz, sib, ynb = place()
    rows = x_ref.shape[0] // PIECES
    has_left, has_right = zz > 0, zz < zs - 1

    barrier = pltpu.get_barrier_semaphore()
    signal(barrier, sib)
    signal(barrier, ynb)
    pl.when(has_left)(lambda: signal(barrier, me - 4))
    pl.when(has_right)(lambda: signal(barrier, me + 4))
    pl.semaphore_wait(barrier, 2 + has_left.astype(jnp.int32) + has_right.astype(jnp.int32))

    own = pltpu.make_async_copy(x_ref, out_ref.at[me], own_sem)
    own.start()

    def copy(kind, shard, j, device, mine=False):
        zt = lax.div(shard, 4)
        slot = zt if kind != SIBLING else zt + zs * lax.rem(lax.div(shard, 2), 2)
        cut = pl.ds(pl.multiple_of(j * rows, rows), rows)
        there = out_ref.at[shard, cut]
        return pltpu.make_async_remote_copy(
            src_ref=x_ref.at[cut] if mine else there,
            dst_ref=there,
            send_sem=send_sem.at[kind * zs + slot, j],
            recv_sem=recv_sem.at[shard, j],
            device_id={"row": device},
            device_id_type=MESH,
        )

    def each(body):
        lax.fori_loop(0, PIECES, lambda j, c: (body(j), c)[1], 0)

    def own_sends(act):
        def body(j):
            pl.when(has_right)(lambda: act(copy(RIGHT, me, j, me + 4, True)))
            pl.when(has_left)(lambda: act(copy(LEFT, me, j, me - 4, True)))
            act(copy(ACROSS, me, j, ynb, True))
            act(copy(SIBLING, me, j, sib, True))

        each(body)

    def along(act, wait):
        for k in range(1, zs):
            for sign in (-1, 1):
                shard = me + sign * 4 * k
                onward = has_right if sign < 0 else has_left
                kind = RIGHT if sign < 0 else LEFT

                def body(j, shard=shard, onward=onward, kind=kind, sign=sign):
                    if wait:
                        copy(SIBLING, shard, j, sib).wait_recv()
                    pl.when(onward)(lambda: act(copy(kind, shard, j, me - sign * 4)))
                    act(copy(ACROSS, shard, j, ynb))
                    act(copy(SIBLING, shard, j, sib))

                pl.when(zz >= k if sign < 0 else zz + k < zs)(functools.partial(each, body))

    def across(act, wait):
        for k in range(zs):
            for sign in (-1, 1):
                if k == 0 and sign == 1:
                    continue
                shard = ynb + sign * 4 * k

                def body(j, shard=shard):
                    if wait:
                        copy(SIBLING, shard, j, sib).wait_recv()
                    act(copy(SIBLING, shard, j, sib))

                pl.when(zz >= k if sign < 0 else zz + k < zs)(functools.partial(each, body))

    start = lambda c: c.start()
    finish = lambda c: c.wait_send()
    own_sends(start)
    along(start, True)
    across(start, True)
    for q in range(2 * zs):
        shard = 2 * q + 1 - core
        each(lambda j, shard=shard: copy(SIBLING, shard, j, sib).wait_recv())
    own.wait()
    own_sends(finish)
    along(finish, False)
    across(finish, False)


def gather(x, row_count):
    zs = row_count // 4
    return pl.pallas_call(
        functools.partial(gather_kernel, zs),
        out_shape=jax.ShapeDtypeStruct((row_count,) + x.shape, x.dtype),
        in_specs=[pl.BlockSpec(memory_space=pl.ANY)],
        out_specs=pl.BlockSpec(memory_space=pl.ANY),
        scratch_shapes=[
            pltpu.SemaphoreType.DMA,
            pltpu.SemaphoreType.DMA((5 * zs, PIECES)),
            pltpu.SemaphoreType.DMA((row_count, PIECES)),
        ],
        compiler_params=pltpu.CompilerParams(collective_id=0, has_side_effects=True),
        name="gather_features",
    )(x)


def layer_kernel(rows_step, lcol, owner, index, flag, x_ref, *refs):
    tiles_row = flag.shape[1]
    far = refs[: rows_step * tiles_row]
    refs = refs[rows_step * tiles_row :]
    weight_ref, grad_ref, lv_ref, rv_ref, hidden_ref, part_ref, base_ref, wg_ref = refs
    first = pl.program_id(0) * rows_step
    blocks_dev, block, feat = x_ref.shape
    lb = lv_ref.shape[1]
    f32, bf16 = jnp.float32, jnp.bfloat16

    @pl.when(first == 0)
    def _():
        base_ref[...] = jnp.zeros_like(base_ref)
        wg_ref[...] = jnp.zeros_like(wg_ref)

        def clear(i, c):
            at = pl.ds(pl.multiple_of(i * 8, 8), 8)
            part_ref[at] = jnp.zeros((8,) + part_ref.shape[1:], bf16)
            return c

        lax.fori_loop(0, part_ref.shape[0] // 8, clear, 0)

    ones = jnp.ones((block, feat), bf16)
    flags = [
        [flag[first + i, t].astype(f32) for t in range(tiles_row)] for i in range(rows_step)
    ]
    rows = [
        jnp.concatenate(
            [lv_ref[i, l] for l in range(lb)] + [rv_ref[i, t] for t in range(tiles_row)], axis=1
        )
        for i in range(rows_step)
    ]
    aggs, norms = [], []
    for i in range(rows_step):
        blocks = [
            jnp.concatenate([x_ref[lcol[first + i, l]], ones], axis=1) for l in range(lb)
        ]
        for t in range(tiles_row):
            seen = jnp.concatenate([far[i * tiles_row + t][0], ones], axis=1)
            blocks.append((seen.astype(f32) * flags[i][t]).astype(bf16))
        total = jnp.dot(rows[i], jnp.concatenate(blocks, axis=0), preferred_element_type=f32)
        aggs.append((x_ref[first + i].astype(f32) + total[:, :feat]).astype(bf16))
        norms.append(lax.rsqrt(1.0 + total[:, feat:]))
    agg = jnp.concatenate(aggs, axis=0)
    norm = jnp.concatenate(norms, axis=0)
    hid = weight_ref.shape[1]
    norm = jnp.concatenate([norm] * (hid // feat), axis=1)
    v = norm * jnp.dot(agg, weight_ref[...], preferred_element_type=f32)
    scale = math.sqrt(2.0 / math.pi)
    square = v * v
    t = jnp.tanh(scale * (v + 0.044715 * (square * v)))
    half = 0.5 * (1.0 + t)
    hidden_ref[...] = (v * half).astype(bf16)
    slope = half + (0.5 * scale) * v * (1.0 - t * t) * (1.0 + (3 * 0.044715) * square)
    gs = (norm * (grad_ref[...].astype(f32) * slope)).astype(bf16)
    dagg = lax.dot_general(
        weight_ref[...], gs, (((1,), (1,)), ((), ())), preferred_element_type=f32
    ).astype(bf16)
    wg_ref[...] += lax.dot_general(agg, gs, (((0,), (0,)), ((), ())), preferred_element_type=f32)
    for i in range(rows_step):
        down = dagg[:, i * block : (i + 1) * block]
        base_ref[first + i] += down.astype(f32)
        terms = jnp.dot(down, rows[i], preferred_element_type=f32)
        for l in range(lb):
            base_ref[lcol[first + i, l]] += terms[:, l * block : (l + 1) * block]
        for t in range(tiles_row):
            at = owner[first + i, t] * blocks_dev + index[first + i, t]
            term = terms[:, (lb + t) * block : (lb + t + 1) * block] * flags[i][t]
            part_ref[at] = (part_ref[at].astype(f32) + term).astype(bf16)


def layer(x, seen, weight, grad_out, local_vals, remote_vals, lcol, owner, index, flag):
    blocks_dev, lb, block, _ = local_vals.shape
    tiles_row = remote_vals.shape[1]
    feat, hid = weight.shape
    rows_step = 4
    whole = lambda *shape: pl.BlockSpec(shape, lambda r, *_: (0,) * len(shape))

    def seen_block(i, t):
        def at(r, lc, ow, ix, fl):
            row = r * rows_step + i
            return ow[row, t] * blocks_dev + ix[row, t], 0, 0

        return pl.BlockSpec((1, block, feat), at)

    far = [seen_block(i, t) for i in range(rows_step) for t in range(tiles_row)]
    return pl.pallas_call(
        functools.partial(layer_kernel, rows_step),
        grid_spec=pltpu.PrefetchScalarGridSpec(
            num_scalar_prefetch=4,
            grid=(blocks_dev // rows_step,),
            in_specs=[whole(blocks_dev, block, feat)]
            + far
            + [
                whole(feat, hid),
                pl.BlockSpec((rows_step * block, hid), lambda r, *_: (r, 0)),
                pl.BlockSpec((rows_step, lb, block, block), lambda r, *_: (r, 0, 0, 0)),
                pl.BlockSpec((rows_step, tiles_row, block, block), lambda r, *_: (r, 0, 0, 0)),
            ],
            out_specs=[
                pl.BlockSpec((rows_step * block, hid), lambda r, *_: (r, 0)),
                whole(seen.shape[0], feat, block),
                whole(blocks_dev, feat, block),
                whole(feat, hid),
            ],
        ),
        out_shape=[
            jax.ShapeDtypeStruct((blocks_dev * block, hid), jnp.bfloat16),
            jax.ShapeDtypeStruct((seen.shape[0], feat, block), jnp.bfloat16),
            jax.ShapeDtypeStruct((blocks_dev, feat, block), jnp.float32),
            jax.ShapeDtypeStruct((feat, hid), jnp.float32),
        ],
        compiler_params=pltpu.CompilerParams(
            dimension_semantics=("arbitrary",), vmem_limit_bytes=48 << 20
        ),
        name="layer",
    )(
        lcol,
        owner,
        index,
        flag,
        x,
        *([seen] * (rows_step * tiles_row)),
        weight,
        grad_out,
        local_vals,
        remote_vals,
    )


def scatter_kernel(
    zs,
    part_ref,
    base_ref,
    w_ref,
    out_ref,
    wout_ref,
    mine,
    from_core,
    from_y,
    from_z,
    held,
    base_sum,
    w_in,
    w_sum,
    load_sem,
    send_sem,
    core_sem,
    y_sem,
    z_sem,
    w_send,
    w_recv,
):
    me, core, yy, zz, sib, ynb = place()
    rows = part_ref.shape[1] // PIECES
    has_left, has_right = zz > 0, zz < zs - 1
    f32, bf16 = jnp.float32, jnp.bfloat16
    near = me + 4 * (1 - 2 * lax.rem(zz, 2))
    apart = me + 8 * (1 - 2 * lax.div(zz, 2))

    def load(zt, yt):
        q = yt * zs + zt
        return pltpu.make_async_copy(
            part_ref.at[zt * 4 + yt * 2 + core], mine.at[q], load_sem.at[q]
        )

    for yt in range(2):
        for zt in range(zs):
            load(zt, yt).start()

    barrier = pltpu.get_barrier_semaphore()
    signal(barrier, sib)
    signal(barrier, ynb)
    signal(barrier, apart)
    pl.when(has_left)(lambda: signal(barrier, me - 4))
    pl.when(has_right)(lambda: signal(barrier, me + 4))
    pl.semaphore_wait(barrier, 3 + has_left.astype(jnp.int32) + has_right.astype(jnp.int32))

    def each(body):
        lax.fori_loop(0, PIECES, lambda j, c: (body(j), c)[1], 0)

    def cut(j):
        return pl.ds(pl.multiple_of(j * rows, rows), rows)

    def remote(src, dst, send, recv, device):
        return pltpu.make_async_remote_copy(
            src_ref=src,
            dst_ref=dst,
            send_sem=send,
            recv_sem=recv,
            device_id={"row": device},
            device_id_type=MESH,
        )

    wrows = w_ref.shape[0] // 2
    kept = pl.ds(pl.multiple_of(core * wrows, wrows), wrows)
    given = pl.ds(pl.multiple_of((1 - core) * wrows, wrows), wrows)
    w_steps = [
        remote(w_ref.at[given], w_in.at[0], w_send.at[0], w_recv.at[0], sib),
        remote(w_sum.at[0], w_in.at[1], w_send.at[1], w_recv.at[1], ynb),
        remote(w_sum.at[1], w_in.at[2], w_send.at[2], w_recv.at[2], near),
        remote(w_sum.at[2], w_in.at[3], w_send.at[3], w_recv.at[3], apart),
    ]
    w_last = remote(wout_ref.at[kept], wout_ref.at[kept], w_send.at[4], w_recv.at[4], sib)
    w_back = remote(wout_ref.at[given], wout_ref.at[given], w_send.at[4], w_recv.at[4], sib)

    def w_go(step):
        w_steps[step].wait_recv()
        held_so_far = w_ref[kept] if step == 0 else w_sum[step - 1]
        total = held_so_far + w_in[step]
        if step < 3:
            w_sum[step] = total
            w_steps[step + 1].start()
        else:
            wout_ref[kept] = total
            w_last.start()

    w_steps[0].start()

    def valid(sign, d):
        return zz >= d if sign < 0 else zz + d < zs

    def order(least):
        for d in range(zs - 1, least - 1, -1):
            for sign in (1, -1) if d else (1,):
                yield d, sign

    def to_core(zt, yt, j):
        return remote(
            part_ref.at[zt * 4 + yt * 2 + 1 - core, cut(j)],
            from_core.at[yt * zs + zt, cut(j)],
            send_sem.at[yt * zs + zt, j],
            core_sem.at[yt * zs + zt, j],
            sib,
        )

    def to_y(zt, j):
        return remote(
            held.at[(1 - yy) * zs + zt, cut(j)],
            from_y.at[zt, cut(j)],
            send_sem.at[2 * zs + zt, j],
            y_sem.at[zt, j],
            ynb,
        )

    def to_z(zt, way, j, device):
        return remote(
            held.at[yy * zs + zt, cut(j)],
            from_z.at[way, zt, cut(j)],
            send_sem.at[3 * zs + zt, j],
            z_sem.at[way, zt, j],
            device,
        )

    for yt in (1 - yy, yy):
        for d, sign in order(0):
            zt = zz + sign * d
            pl.when(valid(sign, d))(
                functools.partial(each, lambda j, zt=zt, yt=yt: to_core(zt, yt, j).start())
            )

    w_go(0)
    step = 1
    for d, sign in order(0):
        zt = zz + sign * d

        @pl.when(valid(sign, d))
        def _(zt=zt):
            q = (1 - yy) * zs + zt
            load(zt, 1 - yy).wait()

            def body(j):
                to_core(zt, 1 - yy, j).wait_recv()
                total = mine[q, cut(j)].astype(f32) + from_core[q, cut(j)].astype(f32)
                held[q, cut(j)] = total.astype(bf16)
                to_y(zt, j).start()

            each(body)

    def summed(zt, j):
        q = yy * zs + zt
        to_core(zt, yy, j).wait_recv()
        to_y(zt, j).wait_recv()
        total = mine[q, cut(j)].astype(f32) + from_core[q, cut(j)].astype(f32)
        return total + from_y[zt, cut(j)].astype(f32)

    w_go(1)
    step = 2
    for d, sign in order(1):
        zt = zz + sign * d
        way = 0 if sign > 0 else 1
        behind = has_left if sign > 0 else has_right

        @pl.when(valid(sign, d))
        def _(zt=zt, way=way, behind=behind, sign=sign):
            load(zt, yy).wait()

            def body(j):
                total = summed(zt, j)
                q = yy * zs + zt

                @pl.when(behind)
                def _():
                    to_z(zt, way, j, me + sign * 4).wait_recv()
                    held[q, cut(j)] = (total + from_z[way, zt, cut(j)].astype(f32)).astype(bf16)

                @pl.when(jnp.logical_not(behind))
                def _():
                    held[q, cut(j)] = total.astype(bf16)

                to_z(zt, way, j, me + sign * 4).start()

            each(body)

        if sign < 0 and step < 4:
            w_go(step)
            step += 1

    load(zz, yy).wait()

    def last(j):
        base_sum[cut(j)] = base_ref[cut(j)] + summed(zz, j)

        @pl.when(has_left)
        def _():
            to_z(zz, 0, j, sib).wait_recv()
            base_sum[cut(j)] += from_z[0, zz, cut(j)].astype(f32)

        @pl.when(has_right)
        def _():
            to_z(zz, 1, j, sib).wait_recv()
            base_sum[cut(j)] += from_z[1, zz, cut(j)].astype(f32)

        out_ref[cut(j)] = base_sum[cut(j)].astype(bf16)

    each(last)

    w_back.wait_recv()
    for c in w_steps:
        c.wait_send()
    w_last.wait_send()
    for zt in range(zs):
        each(lambda j, zt=zt: to_core(zt, 0, j).wait_send())
        each(lambda j, zt=zt: to_core(zt, 1, j).wait_send())
        each(lambda j, zt=zt: to_y(zt, j).wait_send())
        pl.when(zz != zt)(
            functools.partial(each, lambda j, zt=zt: to_z(zt, 0, j, sib).wait_send())
        )


def scatter(part, base, wterm, row_count):
    zs = row_count // 4
    nodes, feat = base.shape
    vmem = pl.BlockSpec(memory_space=pltpu.VMEM)
    dma = pltpu.SemaphoreType.DMA
    shard = lambda *lead: pltpu.VMEM(lead + (nodes, feat), jnp.bfloat16)
    wshape = (wterm.shape[0] // 2, wterm.shape[1])
    return pl.pallas_call(
        functools.partial(scatter_kernel, zs),
        out_shape=[
            jax.ShapeDtypeStruct((nodes, feat), jnp.bfloat16),
            jax.ShapeDtypeStruct(wterm.shape, jnp.float32),
        ],
        in_specs=[pl.BlockSpec(memory_space=pl.ANY), vmem, vmem],
        out_specs=[vmem, vmem],
        scratch_shapes=[
            shard(2 * zs),
            shard(2 * zs),
            shard(zs),
            shard(2, zs),
            shard(2 * zs),
            pltpu.VMEM((nodes, feat), jnp.float32),
            pltpu.VMEM((4,) + wshape, jnp.float32),
            pltpu.VMEM((3,) + wshape, jnp.float32),
            dma((2 * zs,)),
            dma((4 * zs, PIECES)),
            dma((2 * zs, PIECES)),
            dma((zs, PIECES)),
            dma((2, zs, PIECES)),
            dma((5,)),
            dma((5,)),
        ],
        compiler_params=pltpu.CompilerParams(
            collective_id=1, has_side_effects=True, vmem_limit_bytes=48 << 20
        ),
        name="scatter_gradient",
    )(part, base, wterm)


def planned(
    features,
    weight,
    grad_out,
    local_vals,
    local_cols,
    remote_vals,
    remote_owner,
    remote_index,
    remote_flag,
):
    blocks_dev, _, block, _ = local_vals.shape
    nodes, feat = features.shape
    row_count = lax.axis_size("row")
    seen = gather(features, row_count).reshape(row_count * blocks_dev, block, feat)
    hidden, part, base, wterm = layer(
        features.reshape(blocks_dev, block, feat),
        seen,
        weight,
        grad_out,
        local_vals,
        remote_vals,
        local_cols,
        remote_owner,
        remote_index,
        remote_flag,
    )
    back, wsum = scatter(
        part.reshape(row_count, nodes, feat), base.reshape(nodes, feat), wterm, row_count
    )
    input_grad = jnp.swapaxes(back.reshape(blocks_dev, feat, block), 1, 2).reshape(nodes, feat)
    weight_grad = wsum * (1.0 / math.sqrt(nodes * row_count))
    return hidden, input_grad, weight_grad


def solution(mesh):
    return jax.shard_map(
        planned if mesh.shape["row"] == 16 else slotted,
        mesh=mesh,
        in_specs=(
            P(("grp", "row"), None),
            P(),
            P(("grp", "row"), None),
            P(("grp", "row"), None, None, None),
            P(("grp", "row"), None),
            P(("grp", "row"), None, None, None),
            P(("grp", "row"), None),
            P(("grp", "row"), None),
            P(("grp", "row"), None),
        ),
        out_specs=(P(("grp", "row"), None), P(("grp", "row"), None), P("grp", None)),
        check_vma=False,
    )
```

```python
import functools
import math

import jax
import jax.numpy as jnp
from jax import lax
from jax.experimental import pallas as pl
from jax.experimental.pallas import tpu as pltpu
from jax.sharding import PartitionSpec as P


def slotted(
    features,
    weight,
    grad_out,
    local_vals,
    local_cols,
    remote_vals,
    remote_owner,
    remote_index,
    remote_flag,
):
    block_size = local_vals.shape[2]
    blocks_dev = local_vals.shape[0]
    tiles_row = remote_vals.shape[1]
    feat = features.shape[1]
    row_count = lax.axis_size("row")
    slot_cap = max(2, 2 * blocks_dev * tiles_row // row_count)
    tile_count = blocks_dev * tiles_row
    node_count = blocks_dev * block_size
    xblocks = features.reshape(blocks_dev, block_size, feat)
    owners = remote_owner.reshape(-1)
    owner_hot = (owners[:, None] == jnp.arange(row_count, dtype=jnp.int32)[None, :]).astype(
        jnp.int32
    )
    ranks = jnp.sum((jnp.cumsum(owner_hot, axis=0) - owner_hot) * owner_hot, axis=1)
    slot_flat = owners * slot_cap + ranks
    request = (
        jnp.zeros((row_count * slot_cap,), jnp.int32).at[slot_flat].set(remote_index.reshape(-1))
    )
    request = request.reshape(row_count, slot_cap)
    masked = remote_vals * remote_flag[:, :, None, None].astype(jnp.bfloat16)
    tiles_flat = masked.reshape(tile_count, block_size, block_size)
    piece = lax.all_to_all(request, "row", split_axis=0, concat_axis=0, tiled=True)
    found = xblocks[piece]
    returned = lax.all_to_all(found, "row", split_axis=0, concat_axis=0, tiled=True)
    remote_x = returned.reshape(row_count * slot_cap, block_size, feat)[slot_flat]
    remote_sum = jnp.einsum(
        "tij,tjf->tif", tiles_flat, remote_x, preferred_element_type=jnp.float32
    )
    remote_sum = jnp.sum(remote_sum.reshape(blocks_dev, tiles_row, block_size, feat), axis=1)
    local_x = xblocks[local_cols]
    local_sum = jnp.einsum(
        "rlij,rljf->rif", local_vals, local_x, preferred_element_type=jnp.float32
    )
    agg = (
        (xblocks.astype(jnp.float32) + local_sum + remote_sum)
        .reshape(node_count, feat)
        .astype(jnp.bfloat16)
    )
    degree = jnp.sum(local_vals, axis=(1, 3), dtype=jnp.float32) + jnp.sum(
        masked, axis=(1, 3), dtype=jnp.float32
    )
    norm = lax.rsqrt(1.0 + degree.reshape(node_count))
    z_value = norm[:, None] * jnp.dot(agg, weight, preferred_element_type=jnp.float32)
    activated, pull = jax.vjp(jax.nn.gelu, z_value)
    hidden = activated.astype(jnp.bfloat16)
    grad_z = pull(grad_out.astype(jnp.float32))[0]
    scaled_grad = (norm[:, None] * grad_z).astype(jnp.bfloat16)
    weight_term = lax.dot_general(
        agg, scaled_grad, (((0,), (0,)), ((), ())), preferred_element_type=jnp.float32
    )
    total_nodes = node_count * row_count
    weight_grad = lax.psum(weight_term, "row") * (1.0 / math.sqrt(total_nodes))
    dagg = lax.dot_general(
        scaled_grad, weight, (((1,), (1,)), ((), ())), preferred_element_type=jnp.float32
    ).astype(jnp.bfloat16)
    dblocks = dagg.reshape(blocks_dev, block_size, feat)
    local_hot = (
        local_cols[:, :, None] == jnp.arange(blocks_dev, dtype=jnp.int32)[None, None, :]
    ).astype(jnp.float32)
    local_terms = jnp.einsum(
        "rlij,rif->rljf", local_vals, dblocks, preferred_element_type=jnp.float32
    )
    local_back = jnp.einsum("rlk,rljf->kjf", local_hot, local_terms)
    asked_hot = (
        piece[:, :, None] == jnp.arange(blocks_dev, dtype=jnp.int32)[None, None, :]
    ).astype(jnp.bfloat16)
    sender_terms = jnp.einsum(
        "rtij,rif->rtjf", masked, dblocks, preferred_element_type=jnp.float32
    ).astype(jnp.bfloat16)
    part_send = (
        jnp.zeros((row_count * slot_cap, block_size, feat), jnp.bfloat16)
        .at[slot_flat]
        .set(sender_terms.reshape(tile_count, block_size, feat))
    )
    received = lax.all_to_all(
        part_send.reshape(row_count, slot_cap, block_size, feat),
        "row",
        split_axis=0,
        concat_axis=0,
        tiled=True,
    )
    remote_back = jnp.einsum(
        "sck,scjf->kjf", asked_hot, received, preferred_element_type=jnp.float32
    )
    input_grad = (
        (dblocks.astype(jnp.float32) + local_back + remote_back)
        .reshape(node_count, feat)
        .astype(jnp.bfloat16)
    )
    return (hidden, input_grad, weight_grad)


MESH = pl.DeviceIdType.MESH
RIGHT, LEFT, ACROSS, SIBLING = 0, 1, 2, 3
PIECES = 4


def place():
    me = lax.axis_index("row")
    core = lax.rem(me, 2)
    yy = lax.rem(lax.div(me, 2), 2)
    zz = lax.div(me, 4)
    return me, core, yy, zz, me + 1 - 2 * core, me + 2 - 4 * yy


def signal(barrier, device):
    pl.semaphore_signal(barrier, inc=1, device_id={"row": device}, device_id_type=MESH)


def split_rows(nodes):
    last = nodes * 3 // 16
    return (nodes - last) // PIECES, last


def gather_kernel(zs, x_ref, out_ref, own_sem, send_sem, recv_sem):
    me, core, yy, zz, sib, ynb = place()
    rows, tail = split_rows(x_ref.shape[0])
    has_left, has_right = zz > 0, zz < zs - 1

    barrier = pltpu.get_barrier_semaphore()
    signal(barrier, sib)
    signal(barrier, ynb)
    pl.when(has_left)(lambda: signal(barrier, me - 4))
    pl.when(has_right)(lambda: signal(barrier, me + 4))
    pl.semaphore_wait(barrier, 2 + has_left.astype(jnp.int32) + has_right.astype(jnp.int32))

    own = pltpu.make_async_copy(x_ref, out_ref.at[me], own_sem)
    own.start()

    def copy(kind, shard, j, device, mine=False):
        slot = lax.div(shard, 4) + zs * lax.rem(lax.div(shard, 2), 2)
        if j is None:
            cut, j = pl.ds(PIECES * rows, tail), PIECES
        else:
            cut = pl.ds(pl.multiple_of(j * rows, 16), rows)
        there = out_ref.at[shard, cut]
        return pltpu.make_async_remote_copy(
            src_ref=x_ref.at[cut] if mine else there,
            dst_ref=there,
            send_sem=send_sem.at[kind, slot, j],
            recv_sem=recv_sem.at[shard, j],
            device_id={"row": device},
            device_id_type=MESH,
        )

    def each(body):
        lax.fori_loop(0, PIECES, lambda j, c: (body(j), c)[1], 0)

    def valid(sign, k):
        return zz >= k if sign < 0 else zz + k < zs

    def own_sends(act):
        act(copy(ACROSS, me, None, ynb, True))

        def body(j):
            pl.when(has_right)(lambda: act(copy(RIGHT, me, j, me + 4, True)))
            pl.when(has_left)(lambda: act(copy(LEFT, me, j, me - 4, True)))
            act(copy(ACROSS, me, j, ynb, True))
            act(copy(SIBLING, me, j, sib, True))

        each(body)
        act(copy(SIBLING, me, None, sib, True))

    def tails_out(act, k):
        def go(kind, device):
            act(copy(kind, me, None, device, True))
            act(copy(kind, ynb, None, device))

        pl.when(jnp.logical_and(has_right, zz == k))(lambda: go(RIGHT, me + 4))
        pl.when(jnp.logical_and(has_left, zz == zs - 1 - k))(lambda: go(LEFT, me - 4))

    def along(act, wait):
        if wait:
            copy(SIBLING, ynb, None, sib).wait_recv()
        act(copy(SIBLING, ynb, None, sib))
        tails_out(act, 0)
        for k in range(1, zs):
            for sign in (-1, 1):
                shard = me + sign * 4 * k
                onward = has_right if sign < 0 else has_left
                kind = RIGHT if sign < 0 else LEFT

                def body(j, shard=shard, onward=onward, kind=kind, sign=sign):
                    if wait:
                        copy(SIBLING, shard, j, sib).wait_recv()
                    pl.when(onward)(lambda: act(copy(kind, shard, j, me - sign * 4)))
                    act(copy(ACROSS, shard, j, ynb))
                    act(copy(SIBLING, shard, j, sib))

                pl.when(valid(sign, k))(functools.partial(each, body))
            tails_out(act, k)
        for k in range(1, zs):
            for sign in (-1, 1):
                onward = has_right if sign < 0 else has_left
                kind = RIGHT if sign < 0 else LEFT

                @pl.when(valid(sign, k))
                def _(sign=sign, k=k, onward=onward, kind=kind):
                    for base in (me, ynb):
                        shard = base + sign * 4 * k
                        if wait:
                            copy(SIBLING, shard, None, sib).wait_recv()
                        pl.when(onward)(
                            lambda shard=shard: act(copy(kind, shard, None, me - sign * 4))
                        )
                        act(copy(SIBLING, shard, None, sib))

    def across(act, wait):
        for k in range(zs):
            for sign in (-1, 1):
                if k == 0 and sign == 1:
                    continue
                shard = ynb + sign * 4 * k

                def body(j, shard=shard):
                    if wait:
                        copy(SIBLING, shard, j, sib).wait_recv()
                    act(copy(SIBLING, shard, j, sib))

                pl.when(valid(sign, k))(functools.partial(each, body))

    start = lambda c: c.start()
    finish = lambda c: c.wait_send()
    own_sends(start)
    along(start, True)
    across(start, True)
    for q in range(2 * zs):
        shard = 2 * q + 1 - core
        each(lambda j, shard=shard: copy(SIBLING, shard, j, sib).wait_recv())
        copy(SIBLING, shard, None, sib).wait_recv()
    own.wait()
    own_sends(finish)
    along(finish, False)
    across(finish, False)


def gather(x, row_count):
    zs = row_count // 4
    return pl.pallas_call(
        functools.partial(gather_kernel, zs),
        out_shape=jax.ShapeDtypeStruct((row_count,) + x.shape, x.dtype),
        in_specs=[pl.BlockSpec(memory_space=pl.ANY)],
        out_specs=pl.BlockSpec(memory_space=pl.ANY),
        scratch_shapes=[
            pltpu.SemaphoreType.DMA,
            pltpu.SemaphoreType.DMA((4, 2 * zs, PIECES + 1)),
            pltpu.SemaphoreType.DMA((row_count, PIECES + 1)),
        ],
        compiler_params=pltpu.CompilerParams(collective_id=0, has_side_effects=True),
        name="gather_features",
    )(x)


def layer_kernel(rows_step, lcol, owner, index, flag, x_ref, *refs):
    tiles_row = flag.shape[0]
    far = refs[: rows_step * tiles_row]
    refs = refs[rows_step * tiles_row :]
    weight_ref, grad_ref, lv_ref, rv_ref, hidden_ref, part_ref, base_ref, wg_ref = refs
    first = pl.program_id(0) * rows_step
    blocks_dev, block, feat = x_ref.shape
    lb = lv_ref.shape[1]
    f32, bf16 = jnp.float32, jnp.bfloat16

    @pl.when(first == 0)
    def _():
        base_ref[...] = jnp.zeros_like(base_ref)
        wg_ref[...] = jnp.zeros_like(wg_ref)

        def clear(i, c):
            at = pl.ds(pl.multiple_of(i * 8, 8), 8)
            part_ref[at] = jnp.zeros((8,) + part_ref.shape[1:], bf16)
            return c

        lax.fori_loop(0, part_ref.shape[0] // 8, clear, 0)

    ones = jnp.ones((block, feat), bf16)
    flags = [
        [flag[t, first + i].astype(f32) for t in range(tiles_row)] for i in range(rows_step)
    ]
    rows = [
        jnp.concatenate(
            [lv_ref[i, l] for l in range(lb)] + [rv_ref[i, t] for t in range(tiles_row)], axis=1
        )
        for i in range(rows_step)
    ]
    aggs, norms = [], []
    for i in range(rows_step):
        blocks = [
            jnp.concatenate([x_ref[lcol[l, first + i]], ones], axis=1) for l in range(lb)
        ]
        for t in range(tiles_row):
            seen = jnp.concatenate([far[i * tiles_row + t][0], ones], axis=1)
            blocks.append((seen.astype(f32) * flags[i][t]).astype(bf16))
        total = jnp.dot(rows[i], jnp.concatenate(blocks, axis=0), preferred_element_type=f32)
        aggs.append((x_ref[first + i].astype(f32) + total[:, :feat]).astype(bf16))
        norms.append(lax.rsqrt(1.0 + total[:, feat:]))
    agg = jnp.concatenate(aggs, axis=0)
    norm = jnp.concatenate(norms, axis=0)
    hid = weight_ref.shape[1]
    norm = jnp.concatenate([norm] * (hid // feat), axis=1)
    v = norm * jnp.dot(agg, weight_ref[...], preferred_element_type=f32)
    scale = math.sqrt(2.0 / math.pi)
    square = v * v
    t = jnp.tanh(scale * (v + 0.044715 * (square * v)))
    half = 0.5 * (1.0 + t)
    hidden_ref[...] = (v * half).astype(bf16)
    slope = half + (0.5 * scale) * v * (1.0 - t * t) * (1.0 + (3 * 0.044715) * square)
    gs = (norm * (grad_ref[...].astype(f32) * slope)).astype(bf16)
    dagg = lax.dot_general(
        weight_ref[...], gs, (((1,), (1,)), ((), ())), preferred_element_type=f32
    ).astype(bf16)
    wg_ref[...] += lax.dot_general(agg, gs, (((0,), (0,)), ((), ())), preferred_element_type=f32)
    for i in range(rows_step):
        down = dagg[:, i * block : (i + 1) * block]
        base_ref[first + i] += down.astype(f32)
        terms = jnp.dot(down, rows[i], preferred_element_type=f32)
        for l in range(lb):
            base_ref[lcol[l, first + i]] += terms[:, l * block : (l + 1) * block]
        for t in range(tiles_row):
            at = owner[t, first + i] * blocks_dev + index[t, first + i]
            term = terms[:, (lb + t) * block : (lb + t + 1) * block] * flags[i][t]
            part_ref[at] = (part_ref[at].astype(f32) + term).astype(bf16)


def layer(x, seen, weight, grad_out, local_vals, remote_vals, lcol, owner, index, flag):
    blocks_dev, lb, block, _ = local_vals.shape
    tiles_row = remote_vals.shape[1]
    feat, hid = weight.shape
    rows_step = 4
    whole = lambda *shape: pl.BlockSpec(shape, lambda r, *_: (0,) * len(shape))

    def seen_block(i, t):
        def at(r, lc, ow, ix, fl):
            row = r * rows_step + i
            return ow[t, row] * blocks_dev + ix[t, row], 0, 0

        return pl.BlockSpec((1, block, feat), at)

    far = [seen_block(i, t) for i in range(rows_step) for t in range(tiles_row)]
    return pl.pallas_call(
        functools.partial(layer_kernel, rows_step),
        grid_spec=pltpu.PrefetchScalarGridSpec(
            num_scalar_prefetch=4,
            grid=(blocks_dev // rows_step,),
            in_specs=[whole(blocks_dev, block, feat)]
            + far
            + [
                whole(feat, hid),
                pl.BlockSpec((rows_step * block, hid), lambda r, *_: (r, 0)),
                pl.BlockSpec((rows_step, lb, block, block), lambda r, *_: (r, 0, 0, 0)),
                pl.BlockSpec((rows_step, tiles_row, block, block), lambda r, *_: (r, 0, 0, 0)),
            ],
            out_specs=[
                pl.BlockSpec((rows_step * block, hid), lambda r, *_: (r, 0)),
                whole(seen.shape[0], feat, block),
                whole(blocks_dev, feat, block),
                whole(feat, hid),
            ],
        ),
        out_shape=[
            jax.ShapeDtypeStruct((blocks_dev * block, hid), jnp.bfloat16),
            jax.ShapeDtypeStruct((seen.shape[0], feat, block), jnp.bfloat16),
            jax.ShapeDtypeStruct((blocks_dev, feat, block), jnp.float32),
            jax.ShapeDtypeStruct((feat, hid), jnp.float32),
        ],
        compiler_params=pltpu.CompilerParams(
            dimension_semantics=("arbitrary",), vmem_limit_bytes=48 << 20
        ),
        name="layer",
    )(
        lcol,
        owner,
        index,
        flag,
        x,
        *([seen] * (rows_step * tiles_row)),
        weight,
        grad_out,
        local_vals,
        remote_vals,
    )


def scatter_kernel(
    zs,
    part_ref,
    base_ref,
    w_ref,
    out_ref,
    wout_ref,
    mine,
    from_core,
    from_y,
    from_z,
    tail_z,
    held,
    base_sum,
    w_in,
    w_sum,
    load_sem,
    send_sem,
    core_sem,
    y_sem,
    z_sem,
    tail_send,
    tail_sem,
    w_send,
    w_recv,
):
    me, core, yy, zz, sib, ynb = place()
    rows, tail = split_rows(part_ref.shape[1])
    has_left, has_right = zz > 0, zz < zs - 1
    f32, bf16 = jnp.float32, jnp.bfloat16
    near = me + 4 * (1 - 2 * lax.rem(zz, 2))
    apart = me + 8 * (1 - 2 * lax.div(zz, 2))

    def load(zt, yt):
        q = yt * zs + zt
        return pltpu.make_async_copy(
            part_ref.at[zt * 4 + yt * 2 + core], mine.at[q], load_sem.at[q]
        )

    for yt in range(2):
        for zt in range(zs):
            load(zt, yt).start()

    barrier = pltpu.get_barrier_semaphore()
    signal(barrier, sib)
    signal(barrier, ynb)
    signal(barrier, apart)
    pl.when(has_left)(lambda: signal(barrier, me - 4))
    pl.when(has_right)(lambda: signal(barrier, me + 4))
    pl.semaphore_wait(barrier, 3 + has_left.astype(jnp.int32) + has_right.astype(jnp.int32))

    def each(body):
        lax.fori_loop(0, PIECES, lambda j, c: (body(j), c)[1], 0)

    def cut(j):
        if isinstance(j, int):
            return pl.ds(PIECES * rows, tail)
        return pl.ds(pl.multiple_of(j * rows, 16), rows)

    def remote(src, dst, send, recv, device):
        return pltpu.make_async_remote_copy(
            src_ref=src,
            dst_ref=dst,
            send_sem=send,
            recv_sem=recv,
            device_id={"row": device},
            device_id_type=MESH,
        )

    wrows = w_ref.shape[0] // 2
    kept = pl.ds(pl.multiple_of(core * wrows, wrows), wrows)
    given = pl.ds(pl.multiple_of((1 - core) * wrows, wrows), wrows)
    w_steps = [
        remote(w_ref.at[given], w_in.at[0], w_send.at[0], w_recv.at[0], sib),
        remote(w_sum.at[0], w_in.at[1], w_send.at[1], w_recv.at[1], ynb),
        remote(w_sum.at[1], w_in.at[2], w_send.at[2], w_recv.at[2], near),
        remote(w_sum.at[2], w_in.at[3], w_send.at[3], w_recv.at[3], apart),
    ]
    w_last = remote(wout_ref.at[kept], wout_ref.at[kept], w_send.at[4], w_recv.at[4], sib)
    w_back = remote(wout_ref.at[given], wout_ref.at[given], w_send.at[4], w_recv.at[4], sib)

    def w_go(step):
        w_steps[step].wait_recv()
        held_so_far = w_ref[kept] if step == 0 else w_sum[step - 1]
        total = held_so_far + w_in[step]
        if step < 3:
            w_sum[step] = total
            w_steps[step + 1].start()
        else:
            wout_ref[kept] = total
            w_last.start()

    w_steps[0].start()

    def valid(sign, d):
        return zz >= d if sign < 0 else zz + d < zs

    def order(least):
        for d in range(zs - 1, least - 1, -1):
            for sign in (1, -1) if d else (1,):
                yield d, sign

    def to_core(zt, yt, j):
        return remote(
            part_ref.at[zt * 4 + yt * 2 + 1 - core, cut(j)],
            from_core.at[yt * zs + zt, cut(j)],
            send_sem.at[yt * zs + zt, j],
            core_sem.at[yt * zs + zt, j],
            sib,
        )

    def to_y(zt, j):
        return remote(
            held.at[(1 - yy) * zs + zt, cut(j)],
            from_y.at[zt, cut(j)],
            send_sem.at[2 * zs + zt, j],
            y_sem.at[zt, j],
            ynb,
        )

    def to_z(zt, way, j, device):
        return remote(
            held.at[yy * zs + zt, cut(j)],
            from_z.at[way, zt, cut(j)],
            send_sem.at[3 * zs + zt, j],
            z_sem.at[way, zt, j],
            device,
        )

    def to_next(zt, yt, way, device):
        q = yt * zs + zt
        return remote(
            held.at[q, cut(PIECES)],
            tail_z.at[way, q],
            tail_send.at[q],
            tail_sem.at[way, q],
            device,
        )

    def tail_sum(zt, yt):
        q = yt * zs + zt
        to_core(zt, yt, PIECES).wait_recv()
        return mine[q, cut(PIECES)].astype(f32) + from_core[q, cut(PIECES)].astype(f32)

    def core_sends(yt, d, sign):
        zt = zz + sign * d
        pl.when(valid(sign, d))(functools.partial(each, lambda j: to_core(zt, yt, j).start()))

    near_first = list(order(0))
    for d, sign in near_first[:2]:
        core_sends(1 - yy, d, sign)
    for d, sign in near_first:
        zt = zz + sign * d

        @pl.when(valid(sign, d))
        def _(zt=zt):
            to_core(zt, 1 - yy, PIECES).start()
            to_core(zt, yy, PIECES).start()

    for d, sign in near_first[2:]:
        core_sends(1 - yy, d, sign)
    for d, sign in near_first:
        core_sends(yy, d, sign)

    w_go(0)
    for yt in range(2):
        for zt in range(zs):
            load(zt, yt).wait()

    for d in range(zs - 1, -1, -1):
        for sign in (1, -1) if d else (1,):
            zt = zz + sign * d

            @pl.when(valid(sign, d))
            def _(zt=zt):
                q = (1 - yy) * zs + zt

                def body(j):
                    to_core(zt, 1 - yy, j).wait_recv()
                    total = mine[q, cut(j)].astype(f32) + from_core[q, cut(j)].astype(f32)
                    held[q, cut(j)] = total.astype(bf16)
                    to_y(zt, j).start()

                each(body)

        for sign in (1, -1) if d else ():
            zt = zz + sign * d
            way = 0 if sign > 0 else 1
            behind = has_left if sign > 0 else has_right

            @pl.when(valid(sign, d))
            def _(zt=zt, way=way, behind=behind, sign=sign):
                for yt in (1 - yy, yy):
                    q = yt * zs + zt
                    total = tail_sum(zt, yt)

                    @pl.when(behind)
                    def _():
                        to_next(zt, yt, way, sib).wait_recv()
                        held[q, cut(PIECES)] = (total + tail_z[way, q].astype(f32)).astype(bf16)

                    @pl.when(jnp.logical_not(behind))
                    def _():
                        held[q, cut(PIECES)] = total.astype(bf16)

                    to_next(zt, yt, way, me + sign * 4).start()

    for yt in (1 - yy, yy):
        q = yt * zs + zz
        base_sum[cut(PIECES)] = tail_sum(zz, yt)
        for way, behind in ((0, has_left), (1, has_right)):

            @pl.when(behind)
            def _(way=way, q=q, yt=yt):
                to_next(zz, yt, way, sib).wait_recv()
                base_sum[cut(PIECES)] += tail_z[way, q].astype(f32)

        if yt is not yy:
            held[q, cut(PIECES)] = base_sum[cut(PIECES)].astype(bf16)
            to_y(zz, PIECES).start()

    def summed(zt, j):
        q = yy * zs + zt
        to_core(zt, yy, j).wait_recv()
        to_y(zt, j).wait_recv()
        total = mine[q, cut(j)].astype(f32) + from_core[q, cut(j)].astype(f32)
        return total + from_y[zt, cut(j)].astype(f32)

    w_go(1)
    step = 2
    for d, sign in order(1):
        zt = zz + sign * d
        way = 0 if sign > 0 else 1
        behind = has_left if sign > 0 else has_right

        @pl.when(valid(sign, d))
        def _(zt=zt, way=way, behind=behind, sign=sign):

            def body(j):
                total = summed(zt, j)
                q = yy * zs + zt

                @pl.when(behind)
                def _():
                    to_z(zt, way, j, me + sign * 4).wait_recv()
                    held[q, cut(j)] = (total + from_z[way, zt, cut(j)].astype(f32)).astype(bf16)

                @pl.when(jnp.logical_not(behind))
                def _():
                    held[q, cut(j)] = total.astype(bf16)

                to_z(zt, way, j, me + sign * 4).start()

            each(body)

        if sign < 0 and step < 4:
            w_go(step)
            step += 1

    def last(j):
        base_sum[cut(j)] = base_ref[cut(j)] + summed(zz, j)

        @pl.when(has_left)
        def _():
            to_z(zz, 0, j, sib).wait_recv()
            base_sum[cut(j)] += from_z[0, zz, cut(j)].astype(f32)

        @pl.when(has_right)
        def _():
            to_z(zz, 1, j, sib).wait_recv()
            base_sum[cut(j)] += from_z[1, zz, cut(j)].astype(f32)

        out_ref[cut(j)] = base_sum[cut(j)].astype(bf16)

    each(last)
    to_y(zz, PIECES).wait_recv()
    total = base_ref[cut(PIECES)] + base_sum[cut(PIECES)]
    out_ref[cut(PIECES)] = (total + from_y[zz, cut(PIECES)].astype(f32)).astype(bf16)

    w_back.wait_recv()
    for c in w_steps:
        c.wait_send()
    w_last.wait_send()
    to_y(zz, PIECES).wait_send()
    for zt in range(zs):
        for yt in range(2):
            to_core(zt, yt, PIECES).wait_send()
            pl.when(zz != zt)(lambda zt=zt, yt=yt: to_next(zt, yt, 0, sib).wait_send())
        each(lambda j, zt=zt: to_core(zt, 0, j).wait_send())
        each(lambda j, zt=zt: to_core(zt, 1, j).wait_send())
        each(lambda j, zt=zt: to_y(zt, j).wait_send())
        pl.when(zz != zt)(
            functools.partial(each, lambda j, zt=zt: to_z(zt, 0, j, sib).wait_send())
        )


def scatter(part, base, wterm, row_count):
    zs = row_count // 4
    nodes, feat = base.shape
    vmem = pl.BlockSpec(memory_space=pltpu.VMEM)
    dma = pltpu.SemaphoreType.DMA
    shard = lambda *lead: pltpu.VMEM(lead + (nodes, feat), jnp.bfloat16)
    wshape = (wterm.shape[0] // 2, wterm.shape[1])
    return pl.pallas_call(
        functools.partial(scatter_kernel, zs),
        out_shape=[
            jax.ShapeDtypeStruct((nodes, feat), jnp.bfloat16),
            jax.ShapeDtypeStruct(wterm.shape, jnp.float32),
        ],
        in_specs=[pl.BlockSpec(memory_space=pl.ANY), vmem, vmem],
        out_specs=[vmem, vmem],
        scratch_shapes=[
            shard(2 * zs),
            shard(2 * zs),
            shard(zs),
            shard(2, zs),
            pltpu.VMEM((2, 2 * zs, split_rows(nodes)[1], feat), jnp.bfloat16),
            shard(2 * zs),
            pltpu.VMEM((nodes, feat), jnp.float32),
            pltpu.VMEM((4,) + wshape, jnp.float32),
            pltpu.VMEM((3,) + wshape, jnp.float32),
            dma((2 * zs,)),
            dma((4 * zs, PIECES + 1)),
            dma((2 * zs, PIECES + 1)),
            dma((zs, PIECES + 1)),
            dma((2, zs, PIECES)),
            dma((2 * zs,)),
            dma((2, 2 * zs)),
            dma((5,)),
            dma((5,)),
        ],
        compiler_params=pltpu.CompilerParams(
            collective_id=1, has_side_effects=True, vmem_limit_bytes=48 << 20
        ),
        name="scatter_gradient",
    )(part, base, wterm)


def planned(
    features,
    weight,
    grad_out,
    local_vals,
    local_cols,
    remote_vals,
    remote_owner,
    remote_index,
    remote_flag,
):
    blocks_dev, _, block, _ = local_vals.shape
    nodes, feat = features.shape
    row_count = lax.axis_size("row")
    seen = gather(features, row_count).reshape(row_count * blocks_dev, block, feat)
    hidden, part, base, wterm = layer(
        features.reshape(blocks_dev, block, feat),
        seen,
        weight,
        grad_out,
        local_vals,
        remote_vals,
        local_cols.T,
        remote_owner.T,
        remote_index.T,
        remote_flag.T,
    )
    back, wsum = scatter(
        part.reshape(row_count, nodes, feat), base.reshape(nodes, feat), wterm, row_count
    )
    input_grad = jnp.swapaxes(back.reshape(blocks_dev, feat, block), 1, 2).reshape(nodes, feat)
    weight_grad = wsum * (1.0 / math.sqrt(nodes * row_count))
    return hidden, input_grad, weight_grad


def solution(mesh):
    return jax.shard_map(
        planned if mesh.shape["row"] == 16 else slotted,
        mesh=mesh,
        in_specs=(
            P(("grp", "row"), None),
            P(),
            P(("grp", "row"), None),
            P(("grp", "row"), None, None, None),
            P(("grp", "row"), None),
            P(("grp", "row"), None, None, None),
            P(("grp", "row"), None),
            P(("grp", "row"), None),
            P(("grp", "row"), None),
        ),
        out_specs=(P(("grp", "row"), None), P(("grp", "row"), None), P("grp", None)),
        check_vma=False,
    )
```

```python
import functools
import math

import jax
import jax.numpy as jnp
from jax import lax
from jax.experimental import pallas as pl
from jax.experimental.pallas import tpu as pltpu
from jax.sharding import PartitionSpec as P


def slotted(
    features,
    weight,
    grad_out,
    local_vals,
    local_cols,
    remote_vals,
    remote_owner,
    remote_index,
    remote_flag,
):
    block_size = local_vals.shape[2]
    blocks_dev = local_vals.shape[0]
    tiles_row = remote_vals.shape[1]
    feat = features.shape[1]
    row_count = lax.axis_size("row")
    slot_cap = max(2, 2 * blocks_dev * tiles_row // row_count)
    tile_count = blocks_dev * tiles_row
    node_count = blocks_dev * block_size
    xblocks = features.reshape(blocks_dev, block_size, feat)
    owners = remote_owner.reshape(-1)
    owner_hot = (owners[:, None] == jnp.arange(row_count, dtype=jnp.int32)[None, :]).astype(
        jnp.int32
    )
    ranks = jnp.sum((jnp.cumsum(owner_hot, axis=0) - owner_hot) * owner_hot, axis=1)
    slot_flat = owners * slot_cap + ranks
    request = (
        jnp.zeros((row_count * slot_cap,), jnp.int32).at[slot_flat].set(remote_index.reshape(-1))
    )
    request = request.reshape(row_count, slot_cap)
    masked = remote_vals * remote_flag[:, :, None, None].astype(jnp.bfloat16)
    tiles_flat = masked.reshape(tile_count, block_size, block_size)
    piece = lax.all_to_all(request, "row", split_axis=0, concat_axis=0, tiled=True)
    found = xblocks[piece]
    returned = lax.all_to_all(found, "row", split_axis=0, concat_axis=0, tiled=True)
    remote_x = returned.reshape(row_count * slot_cap, block_size, feat)[slot_flat]
    remote_sum = jnp.einsum(
        "tij,tjf->tif", tiles_flat, remote_x, preferred_element_type=jnp.float32
    )
    remote_sum = jnp.sum(remote_sum.reshape(blocks_dev, tiles_row, block_size, feat), axis=1)
    local_x = xblocks[local_cols]
    local_sum = jnp.einsum(
        "rlij,rljf->rif", local_vals, local_x, preferred_element_type=jnp.float32
    )
    agg = (
        (xblocks.astype(jnp.float32) + local_sum + remote_sum)
        .reshape(node_count, feat)
        .astype(jnp.bfloat16)
    )
    degree = jnp.sum(local_vals, axis=(1, 3), dtype=jnp.float32) + jnp.sum(
        masked, axis=(1, 3), dtype=jnp.float32
    )
    norm = lax.rsqrt(1.0 + degree.reshape(node_count))
    z_value = norm[:, None] * jnp.dot(agg, weight, preferred_element_type=jnp.float32)
    activated, pull = jax.vjp(jax.nn.gelu, z_value)
    hidden = activated.astype(jnp.bfloat16)
    grad_z = pull(grad_out.astype(jnp.float32))[0]
    scaled_grad = (norm[:, None] * grad_z).astype(jnp.bfloat16)
    weight_term = lax.dot_general(
        agg, scaled_grad, (((0,), (0,)), ((), ())), preferred_element_type=jnp.float32
    )
    total_nodes = node_count * row_count
    weight_grad = lax.psum(weight_term, "row") * (1.0 / math.sqrt(total_nodes))
    dagg = lax.dot_general(
        scaled_grad, weight, (((1,), (1,)), ((), ())), preferred_element_type=jnp.float32
    ).astype(jnp.bfloat16)
    dblocks = dagg.reshape(blocks_dev, block_size, feat)
    local_hot = (
        local_cols[:, :, None] == jnp.arange(blocks_dev, dtype=jnp.int32)[None, None, :]
    ).astype(jnp.float32)
    local_terms = jnp.einsum(
        "rlij,rif->rljf", local_vals, dblocks, preferred_element_type=jnp.float32
    )
    local_back = jnp.einsum("rlk,rljf->kjf", local_hot, local_terms)
    asked_hot = (
        piece[:, :, None] == jnp.arange(blocks_dev, dtype=jnp.int32)[None, None, :]
    ).astype(jnp.bfloat16)
    sender_terms = jnp.einsum(
        "rtij,rif->rtjf", masked, dblocks, preferred_element_type=jnp.float32
    ).astype(jnp.bfloat16)
    part_send = (
        jnp.zeros((row_count * slot_cap, block_size, feat), jnp.bfloat16)
        .at[slot_flat]
        .set(sender_terms.reshape(tile_count, block_size, feat))
    )
    received = lax.all_to_all(
        part_send.reshape(row_count, slot_cap, block_size, feat),
        "row",
        split_axis=0,
        concat_axis=0,
        tiled=True,
    )
    remote_back = jnp.einsum(
        "sck,scjf->kjf", asked_hot, received, preferred_element_type=jnp.float32
    )
    input_grad = (
        (dblocks.astype(jnp.float32) + local_back + remote_back)
        .reshape(node_count, feat)
        .astype(jnp.bfloat16)
    )
    return (hidden, input_grad, weight_grad)


MESH = pl.DeviceIdType.MESH
RIGHT, LEFT, ACROSS, SIBLING = 0, 1, 2, 3
PIECES = 4


def place():
    me = lax.axis_index("row")
    core = lax.rem(me, 2)
    yy = lax.rem(lax.div(me, 2), 2)
    zz = lax.div(me, 4)
    return me, core, yy, zz, me + 1 - 2 * core, me + 2 - 4 * yy


def signal(barrier, device):
    pl.semaphore_signal(barrier, inc=1, device_id={"row": device}, device_id_type=MESH)


def split_rows(nodes):
    last = nodes // 8
    return (nodes - last) // PIECES, last


def gather_kernel(zs, x_ref, out_ref, own_sem, send_sem, recv_sem):
    me, core, yy, zz, sib, ynb = place()
    rows, tail = split_rows(x_ref.shape[0])
    has_left, has_right = zz > 0, zz < zs - 1

    barrier = pltpu.get_barrier_semaphore()
    signal(barrier, sib)
    signal(barrier, ynb)
    pl.when(has_left)(lambda: signal(barrier, me - 4))
    pl.when(has_right)(lambda: signal(barrier, me + 4))
    pl.semaphore_wait(barrier, 2 + has_left.astype(jnp.int32) + has_right.astype(jnp.int32))

    own = pltpu.make_async_copy(x_ref, out_ref.at[me], own_sem)
    own.start()

    def copy(kind, shard, j, device, mine=False):
        slot = lax.div(shard, 4) + zs * lax.rem(lax.div(shard, 2), 2)
        if j is None:
            cut, j = pl.ds(PIECES * rows, tail), PIECES
        else:
            cut = pl.ds(pl.multiple_of(j * rows, 16), rows)
        there = out_ref.at[shard, cut]
        return pltpu.make_async_remote_copy(
            src_ref=x_ref.at[cut] if mine else there,
            dst_ref=there,
            send_sem=send_sem.at[kind, slot, j],
            recv_sem=recv_sem.at[shard, j],
            device_id={"row": device},
            device_id_type=MESH,
        )

    def each(body):
        lax.fori_loop(0, PIECES, lambda j, c: (body(j), c)[1], 0)

    def valid(sign, k):
        return zz >= k if sign < 0 else zz + k < zs

    def own_sends(act):
        act(copy(ACROSS, me, None, ynb, True))

        def body(j):
            pl.when(has_right)(lambda: act(copy(RIGHT, me, j, me + 4, True)))
            pl.when(has_left)(lambda: act(copy(LEFT, me, j, me - 4, True)))
            act(copy(ACROSS, me, j, ynb, True))
            act(copy(SIBLING, me, j, sib, True))

        each(body)
        act(copy(SIBLING, me, None, sib, True))

    def tails_out(act, k):
        def go(kind, device):
            act(copy(kind, me, None, device, True))
            act(copy(kind, ynb, None, device))

        pl.when(jnp.logical_and(has_right, zz == k))(lambda: go(RIGHT, me + 4))
        pl.when(jnp.logical_and(has_left, zz == zs - 1 - k))(lambda: go(LEFT, me - 4))

    def along(act, wait):
        if wait:
            copy(SIBLING, ynb, None, sib).wait_recv()
        act(copy(SIBLING, ynb, None, sib))
        tails_out(act, 0)
        for k in range(1, zs):
            for sign in (-1, 1):
                shard = me + sign * 4 * k
                onward = has_right if sign < 0 else has_left
                kind = RIGHT if sign < 0 else LEFT

                def body(j, shard=shard, onward=onward, kind=kind, sign=sign):
                    if wait:
                        copy(SIBLING, shard, j, sib).wait_recv()
                    pl.when(onward)(lambda: act(copy(kind, shard, j, me - sign * 4)))
                    act(copy(ACROSS, shard, j, ynb))
                    act(copy(SIBLING, shard, j, sib))

                pl.when(valid(sign, k))(functools.partial(each, body))
            tails_out(act, k)
        for k in range(1, zs):
            for sign in (-1, 1):
                onward = has_right if sign < 0 else has_left
                kind = RIGHT if sign < 0 else LEFT

                @pl.when(valid(sign, k))
                def _(sign=sign, k=k, onward=onward, kind=kind):
                    for base in (me, ynb):
                        shard = base + sign * 4 * k
                        if wait:
                            copy(SIBLING, shard, None, sib).wait_recv()
                        pl.when(onward)(
                            lambda shard=shard: act(copy(kind, shard, None, me - sign * 4))
                        )
                        act(copy(SIBLING, shard, None, sib))

    def across(act, wait):
        for k in range(zs):
            for sign in (-1, 1):
                if k == 0 and sign == 1:
                    continue
                shard = ynb + sign * 4 * k

                def body(j, shard=shard):
                    if wait:
                        copy(SIBLING, shard, j, sib).wait_recv()
                    act(copy(SIBLING, shard, j, sib))

                pl.when(valid(sign, k))(functools.partial(each, body))

    start = lambda c: c.start()
    finish = lambda c: c.wait_send()
    own_sends(start)
    along(start, True)
    across(start, True)
    for q in range(2 * zs):
        shard = 2 * q + 1 - core
        each(lambda j, shard=shard: copy(SIBLING, shard, j, sib).wait_recv())
        copy(SIBLING, shard, None, sib).wait_recv()
    own.wait()
    own_sends(finish)
    along(finish, False)
    across(finish, False)


def gather(x, row_count):
    zs = row_count // 4
    return pl.pallas_call(
        functools.partial(gather_kernel, zs),
        out_shape=jax.ShapeDtypeStruct((row_count,) + x.shape, x.dtype),
        in_specs=[pl.BlockSpec(memory_space=pl.ANY)],
        out_specs=pl.BlockSpec(memory_space=pl.ANY),
        scratch_shapes=[
            pltpu.SemaphoreType.DMA,
            pltpu.SemaphoreType.DMA((4, 2 * zs, PIECES + 1)),
            pltpu.SemaphoreType.DMA((row_count, PIECES + 1)),
        ],
        compiler_params=pltpu.CompilerParams(collective_id=0, has_side_effects=True),
        name="gather_features",
    )(x)


def layer_kernel(rows_step, lcol, owner, index, flag, x_ref, *refs):
    tiles_row = flag.shape[0]
    far = refs[: rows_step * tiles_row]
    refs = refs[rows_step * tiles_row :]
    weight_ref, grad_ref, lv_ref, rv_ref, hidden_ref, part_ref, base_ref, wg_ref = refs
    first = pl.program_id(0) * rows_step
    blocks_dev, block, feat = x_ref.shape
    lb = lv_ref.shape[1]
    f32, bf16 = jnp.float32, jnp.bfloat16

    @pl.when(first == 0)
    def _():
        base_ref[...] = jnp.zeros_like(base_ref)
        wg_ref[...] = jnp.zeros_like(wg_ref)

        def clear(i, c):
            at = pl.ds(pl.multiple_of(i * 8, 8), 8)
            part_ref[at] = jnp.zeros((8,) + part_ref.shape[1:], bf16)
            return c

        lax.fori_loop(0, part_ref.shape[0] // 8, clear, 0)

    ones = jnp.ones((block, feat), bf16)
    flags = [
        [flag[t, first + i].astype(f32) for t in range(tiles_row)] for i in range(rows_step)
    ]
    rows = [
        jnp.concatenate(
            [lv_ref[i, l] for l in range(lb)] + [rv_ref[i, t] for t in range(tiles_row)], axis=1
        )
        for i in range(rows_step)
    ]
    aggs, norms = [], []
    for i in range(rows_step):
        blocks = [
            jnp.concatenate([x_ref[lcol[l, first + i]], ones], axis=1) for l in range(lb)
        ]
        for t in range(tiles_row):
            seen = jnp.concatenate([far[i * tiles_row + t][0], ones], axis=1)
            blocks.append((seen.astype(f32) * flags[i][t]).astype(bf16))
        total = jnp.dot(rows[i], jnp.concatenate(blocks, axis=0), preferred_element_type=f32)
        aggs.append((x_ref[first + i].astype(f32) + total[:, :feat]).astype(bf16))
        norms.append(lax.rsqrt(1.0 + total[:, feat:]))
    agg = jnp.concatenate(aggs, axis=0)
    norm = jnp.concatenate(norms, axis=0)
    hid = weight_ref.shape[1]
    norm = jnp.concatenate([norm] * (hid // feat), axis=1)
    v = norm * jnp.dot(agg, weight_ref[...], preferred_element_type=f32)
    scale = math.sqrt(2.0 / math.pi)
    square = v * v
    t = jnp.tanh(scale * (v + 0.044715 * (square * v)))
    half = 0.5 * (1.0 + t)
    hidden_ref[...] = (v * half).astype(bf16)
    slope = half + (0.5 * scale) * v * (1.0 - t * t) * (1.0 + (3 * 0.044715) * square)
    gs = (norm * (grad_ref[...].astype(f32) * slope)).astype(bf16)
    dagg = lax.dot_general(
        weight_ref[...], gs, (((1,), (1,)), ((), ())), preferred_element_type=f32
    ).astype(bf16)
    wg_ref[...] += lax.dot_general(agg, gs, (((0,), (0,)), ((), ())), preferred_element_type=f32)
    for i in range(rows_step):
        down = dagg[:, i * block : (i + 1) * block]
        base_ref[first + i] += down.astype(f32)
        terms = jnp.dot(down, rows[i], preferred_element_type=f32)
        for l in range(lb):
            base_ref[lcol[l, first + i]] += terms[:, l * block : (l + 1) * block]
        for t in range(tiles_row):
            at = owner[t, first + i] * blocks_dev + index[t, first + i]
            term = terms[:, (lb + t) * block : (lb + t + 1) * block] * flags[i][t]
            part_ref[at] = (part_ref[at].astype(f32) + term).astype(bf16)


def layer(x, seen, weight, grad_out, local_vals, remote_vals, lcol, owner, index, flag):
    blocks_dev, lb, block, _ = local_vals.shape
    tiles_row = remote_vals.shape[1]
    feat, hid = weight.shape
    rows_step = 4
    whole = lambda *shape: pl.BlockSpec(shape, lambda r, *_: (0,) * len(shape))

    def seen_block(i, t):
        def at(r, lc, ow, ix, fl):
            row = r * rows_step + i
            return ow[t, row] * blocks_dev + ix[t, row], 0, 0

        return pl.BlockSpec((1, block, feat), at)

    far = [seen_block(i, t) for i in range(rows_step) for t in range(tiles_row)]
    return pl.pallas_call(
        functools.partial(layer_kernel, rows_step),
        grid_spec=pltpu.PrefetchScalarGridSpec(
            num_scalar_prefetch=4,
            grid=(blocks_dev // rows_step,),
            in_specs=[whole(blocks_dev, block, feat)]
            + far
            + [
                whole(feat, hid),
                pl.BlockSpec((rows_step * block, hid), lambda r, *_: (r, 0)),
                pl.BlockSpec((rows_step, lb, block, block), lambda r, *_: (r, 0, 0, 0)),
                pl.BlockSpec((rows_step, tiles_row, block, block), lambda r, *_: (r, 0, 0, 0)),
            ],
            out_specs=[
                pl.BlockSpec((rows_step * block, hid), lambda r, *_: (r, 0)),
                whole(seen.shape[0], feat, block),
                whole(blocks_dev, feat, block),
                whole(feat, hid),
            ],
        ),
        out_shape=[
            jax.ShapeDtypeStruct((blocks_dev * block, hid), jnp.bfloat16),
            jax.ShapeDtypeStruct((seen.shape[0], feat, block), jnp.bfloat16),
            jax.ShapeDtypeStruct((blocks_dev, feat, block), jnp.float32),
            jax.ShapeDtypeStruct((feat, hid), jnp.float32),
        ],
        compiler_params=pltpu.CompilerParams(
            dimension_semantics=("arbitrary",), vmem_limit_bytes=28 << 20
        ),
        name="layer",
    )(
        lcol,
        owner,
        index,
        flag,
        x,
        *([seen] * (rows_step * tiles_row)),
        weight,
        grad_out,
        local_vals,
        remote_vals,
    )


def scatter_kernel(
    zs,
    part_ref,
    base_ref,
    w_ref,
    out_ref,
    wout_ref,
    mine,
    from_core,
    from_y,
    from_z,
    tail_z,
    held,
    base_sum,
    w_in,
    w_sum,
    load_sem,
    send_sem,
    core_sem,
    y_sem,
    z_sem,
    tail_send,
    tail_sem,
    w_send,
    w_recv,
):
    me, core, yy, zz, sib, ynb = place()
    rows, tail = split_rows(part_ref.shape[1])
    has_left, has_right = zz > 0, zz < zs - 1
    f32, bf16 = jnp.float32, jnp.bfloat16
    near = me + 4 * (1 - 2 * lax.rem(zz, 2))
    apart = me + 8 * (1 - 2 * lax.div(zz, 2))

    def load(zt, yt):
        q = yt * zs + zt
        return pltpu.make_async_copy(
            part_ref.at[zt * 4 + yt * 2 + core], mine.at[q], load_sem.at[q]
        )

    for yt in range(2):
        for zt in range(zs):
            load(zt, yt).start()

    barrier = pltpu.get_barrier_semaphore()
    signal(barrier, sib)
    signal(barrier, ynb)
    signal(barrier, apart)
    pl.when(has_left)(lambda: signal(barrier, me - 4))
    pl.when(has_right)(lambda: signal(barrier, me + 4))
    pl.semaphore_wait(barrier, 3 + has_left.astype(jnp.int32) + has_right.astype(jnp.int32))

    def each(body):
        lax.fori_loop(0, PIECES, lambda j, c: (body(j), c)[1], 0)

    def cut(j):
        if isinstance(j, int):
            return pl.ds(PIECES * rows, tail)
        return pl.ds(pl.multiple_of(j * rows, 16), rows)

    def remote(src, dst, send, recv, device):
        return pltpu.make_async_remote_copy(
            src_ref=src,
            dst_ref=dst,
            send_sem=send,
            recv_sem=recv,
            device_id={"row": device},
            device_id_type=MESH,
        )

    wrows = w_ref.shape[0] // 2
    kept = pl.ds(pl.multiple_of(core * wrows, wrows), wrows)
    given = pl.ds(pl.multiple_of((1 - core) * wrows, wrows), wrows)
    w_steps = [
        remote(w_ref.at[given], w_in.at[0], w_send.at[0], w_recv.at[0], sib),
        remote(w_sum.at[0], w_in.at[1], w_send.at[1], w_recv.at[1], ynb),
        remote(w_sum.at[1], w_in.at[2], w_send.at[2], w_recv.at[2], near),
        remote(w_sum.at[2], w_in.at[3], w_send.at[3], w_recv.at[3], apart),
    ]
    w_last = remote(wout_ref.at[kept], wout_ref.at[kept], w_send.at[4], w_recv.at[4], sib)
    w_back = remote(wout_ref.at[given], wout_ref.at[given], w_send.at[4], w_recv.at[4], sib)

    def w_go(step):
        w_steps[step].wait_recv()
        held_so_far = w_ref[kept] if step == 0 else w_sum[step - 1]
        total = held_so_far + w_in[step]
        if step < 3:
            w_sum[step] = total
            w_steps[step + 1].start()
        else:
            wout_ref[kept] = total
            w_last.start()

    w_steps[0].start()

    def valid(sign, d):
        return zz >= d if sign < 0 else zz + d < zs

    def order(least):
        for d in range(zs - 1, least - 1, -1):
            for sign in (1, -1) if d else (1,):
                yield d, sign

    def to_core(zt, yt, j):
        return remote(
            part_ref.at[zt * 4 + yt * 2 + 1 - core, cut(j)],
            from_core.at[yt * zs + zt, cut(j)],
            send_sem.at[yt * zs + zt, j],
            core_sem.at[yt * zs + zt, j],
            sib,
        )

    def to_y(zt, j):
        return remote(
            held.at[(1 - yy) * zs + zt, cut(j)],
            from_y.at[zt, cut(j)],
            send_sem.at[2 * zs + zt, j],
            y_sem.at[zt, j],
            ynb,
        )

    def to_z(zt, way, j, device):
        return remote(
            held.at[yy * zs + zt, cut(j)],
            from_z.at[way, zt, cut(j)],
            send_sem.at[3 * zs + zt, j],
            z_sem.at[way, zt, j],
            device,
        )

    def to_next(zt, yt, way, device):
        q = yt * zs + zt
        return remote(
            held.at[q, cut(PIECES)],
            tail_z.at[way, q],
            tail_send.at[q],
            tail_sem.at[way, q],
            device,
        )

    def tail_sum(zt, yt):
        q = yt * zs + zt
        to_core(zt, yt, PIECES).wait_recv()
        return mine[q, cut(PIECES)].astype(f32) + from_core[q, cut(PIECES)].astype(f32)

    def core_sends(yt, d, sign):
        zt = zz + sign * d
        pl.when(valid(sign, d))(functools.partial(each, lambda j: to_core(zt, yt, j).start()))

    near_first = list(order(0))
    for d, sign in near_first[:2]:
        core_sends(1 - yy, d, sign)
    for d, sign in near_first:
        zt = zz + sign * d

        @pl.when(valid(sign, d))
        def _(zt=zt):
            to_core(zt, 1 - yy, PIECES).start()
            to_core(zt, yy, PIECES).start()

    for d, sign in near_first[2:]:
        core_sends(1 - yy, d, sign)
    for d, sign in near_first:
        core_sends(yy, d, sign)

    w_go(0)
    for yt in range(2):
        for zt in range(zs):
            load(zt, yt).wait()

    for d in range(zs - 1, -1, -1):
        for sign in (1, -1) if d else (1,):
            zt = zz + sign * d

            @pl.when(valid(sign, d))
            def _(zt=zt):
                q = (1 - yy) * zs + zt

                def body(j):
                    to_core(zt, 1 - yy, j).wait_recv()
                    total = mine[q, cut(j)].astype(f32) + from_core[q, cut(j)].astype(f32)
                    held[q, cut(j)] = total.astype(bf16)
                    to_y(zt, j).start()

                each(body)

        for sign in (1, -1) if d else ():
            zt = zz + sign * d
            way = 0 if sign > 0 else 1
            behind = has_left if sign > 0 else has_right

            @pl.when(valid(sign, d))
            def _(zt=zt, way=way, behind=behind, sign=sign):
                for yt in (1 - yy, yy):
                    q = yt * zs + zt
                    total = tail_sum(zt, yt)

                    @pl.when(behind)
                    def _():
                        to_next(zt, yt, way, sib).wait_recv()
                        held[q, cut(PIECES)] = (total + tail_z[way, q].astype(f32)).astype(bf16)

                    @pl.when(jnp.logical_not(behind))
                    def _():
                        held[q, cut(PIECES)] = total.astype(bf16)

                    to_next(zt, yt, way, me + sign * 4).start()

    for yt in (1 - yy, yy):
        q = yt * zs + zz
        base_sum[cut(PIECES)] = tail_sum(zz, yt)
        for way, behind in ((0, has_left), (1, has_right)):

            @pl.when(behind)
            def _(way=way, q=q, yt=yt):
                to_next(zz, yt, way, sib).wait_recv()
                base_sum[cut(PIECES)] += tail_z[way, q].astype(f32)

        if yt is not yy:
            held[q, cut(PIECES)] = base_sum[cut(PIECES)].astype(bf16)
            to_y(zz, PIECES).start()

    def summed(zt, j):
        q = yy * zs + zt
        to_core(zt, yy, j).wait_recv()
        to_y(zt, j).wait_recv()
        total = mine[q, cut(j)].astype(f32) + from_core[q, cut(j)].astype(f32)
        return total + from_y[zt, cut(j)].astype(f32)

    w_go(1)
    step = 2
    for d, sign in order(1):
        zt = zz + sign * d
        way = 0 if sign > 0 else 1
        behind = has_left if sign > 0 else has_right

        @pl.when(valid(sign, d))
        def _(zt=zt, way=way, behind=behind, sign=sign):

            def body(j):
                total = summed(zt, j)
                q = yy * zs + zt

                @pl.when(behind)
                def _():
                    to_z(zt, way, j, me + sign * 4).wait_recv()
                    held[q, cut(j)] = (total + from_z[way, zt, cut(j)].astype(f32)).astype(bf16)

                @pl.when(jnp.logical_not(behind))
                def _():
                    held[q, cut(j)] = total.astype(bf16)

                to_z(zt, way, j, me + sign * 4).start()

            each(body)

        if sign < 0 and step < 4:
            w_go(step)
            step += 1

    def last(j):
        base_sum[cut(j)] = base_ref[cut(j)] + summed(zz, j)

        @pl.when(has_left)
        def _():
            to_z(zz, 0, j, sib).wait_recv()
            base_sum[cut(j)] += from_z[0, zz, cut(j)].astype(f32)

        @pl.when(has_right)
        def _():
            to_z(zz, 1, j, sib).wait_recv()
            base_sum[cut(j)] += from_z[1, zz, cut(j)].astype(f32)

        out_ref[cut(j)] = base_sum[cut(j)].astype(bf16)

    each(last)
    to_y(zz, PIECES).wait_recv()
    total = base_ref[cut(PIECES)] + base_sum[cut(PIECES)]
    out_ref[cut(PIECES)] = (total + from_y[zz, cut(PIECES)].astype(f32)).astype(bf16)

    w_back.wait_recv()
    for c in w_steps:
        c.wait_send()
    w_last.wait_send()
    to_y(zz, PIECES).wait_send()
    for zt in range(zs):
        for yt in range(2):
            to_core(zt, yt, PIECES).wait_send()
            pl.when(zz != zt)(lambda zt=zt, yt=yt: to_next(zt, yt, 0, sib).wait_send())
        each(lambda j, zt=zt: to_core(zt, 0, j).wait_send())
        each(lambda j, zt=zt: to_core(zt, 1, j).wait_send())
        each(lambda j, zt=zt: to_y(zt, j).wait_send())
        pl.when(zz != zt)(
            functools.partial(each, lambda j, zt=zt: to_z(zt, 0, j, sib).wait_send())
        )


def scatter(part, base, wterm, row_count):
    zs = row_count // 4
    nodes, feat = base.shape
    vmem = pl.BlockSpec(memory_space=pltpu.VMEM)
    dma = pltpu.SemaphoreType.DMA
    shard = lambda *lead: pltpu.VMEM(lead + (nodes, feat), jnp.bfloat16)
    wshape = (wterm.shape[0] // 2, wterm.shape[1])
    return pl.pallas_call(
        functools.partial(scatter_kernel, zs),
        out_shape=[
            jax.ShapeDtypeStruct((nodes, feat), jnp.bfloat16),
            jax.ShapeDtypeStruct(wterm.shape, jnp.float32),
        ],
        in_specs=[pl.BlockSpec(memory_space=pl.ANY), vmem, vmem],
        out_specs=[vmem, vmem],
        scratch_shapes=[
            shard(2 * zs),
            shard(2 * zs),
            shard(zs),
            shard(2, zs),
            pltpu.VMEM((2, 2 * zs, split_rows(nodes)[1], feat), jnp.bfloat16),
            shard(2 * zs),
            pltpu.VMEM((nodes, feat), jnp.float32),
            pltpu.VMEM((4,) + wshape, jnp.float32),
            pltpu.VMEM((3,) + wshape, jnp.float32),
            dma((2 * zs,)),
            dma((4 * zs, PIECES + 1)),
            dma((2 * zs, PIECES + 1)),
            dma((zs, PIECES + 1)),
            dma((2, zs, PIECES)),
            dma((2 * zs,)),
            dma((2, 2 * zs)),
            dma((5,)),
            dma((5,)),
        ],
        compiler_params=pltpu.CompilerParams(
            collective_id=1, has_side_effects=True, vmem_limit_bytes=24 << 20
        ),
        name="scatter_gradient",
    )(part, base, wterm)


def planned(
    features,
    weight,
    grad_out,
    local_vals,
    local_cols,
    remote_vals,
    remote_owner,
    remote_index,
    remote_flag,
):
    blocks_dev, _, block, _ = local_vals.shape
    nodes, feat = features.shape
    row_count = lax.axis_size("row")
    seen = gather(features, row_count).reshape(row_count * blocks_dev, block, feat)
    hidden, part, base, wterm = layer(
        features.reshape(blocks_dev, block, feat),
        seen,
        weight,
        grad_out,
        local_vals,
        remote_vals,
        local_cols.T,
        remote_owner.T,
        remote_index.T,
        remote_flag.T,
    )
    back, wsum = scatter(
        part.reshape(row_count, nodes, feat), base.reshape(nodes, feat), wterm, row_count
    )
    input_grad = jnp.swapaxes(back.reshape(blocks_dev, feat, block), 1, 2).reshape(nodes, feat)
    weight_grad = wsum * (1.0 / math.sqrt(nodes * row_count))
    return hidden, input_grad, weight_grad


def solution(mesh):
    return jax.shard_map(
        planned if mesh.shape["row"] == 16 else slotted,
        mesh=mesh,
        in_specs=(
            P(("grp", "row"), None),
            P(),
            P(("grp", "row"), None),
            P(("grp", "row"), None, None, None),
            P(("grp", "row"), None),
            P(("grp", "row"), None, None, None),
            P(("grp", "row"), None),
            P(("grp", "row"), None),
            P(("grp", "row"), None),
        ),
        out_specs=(P(("grp", "row"), None), P(("grp", "row"), None), P("grp", None)),
        check_vma=False,
    )
```

```python
import functools
import math

import jax
import jax.numpy as jnp
from jax import lax
from jax.experimental import pallas as pl
from jax.experimental.pallas import tpu as pltpu
from jax.sharding import PartitionSpec as P


def slotted(
    features,
    weight,
    grad_out,
    local_vals,
    local_cols,
    remote_vals,
    remote_owner,
    remote_index,
    remote_flag,
):
    block_size = local_vals.shape[2]
    blocks_dev = local_vals.shape[0]
    tiles_row = remote_vals.shape[1]
    feat = features.shape[1]
    row_count = lax.axis_size("row")
    slot_cap = max(2, 2 * blocks_dev * tiles_row // row_count)
    tile_count = blocks_dev * tiles_row
    node_count = blocks_dev * block_size
    xblocks = features.reshape(blocks_dev, block_size, feat)
    owners = remote_owner.reshape(-1)
    owner_hot = (owners[:, None] == jnp.arange(row_count, dtype=jnp.int32)[None, :]).astype(
        jnp.int32
    )
    ranks = jnp.sum((jnp.cumsum(owner_hot, axis=0) - owner_hot) * owner_hot, axis=1)
    slot_flat = owners * slot_cap + ranks
    request = (
        jnp.zeros((row_count * slot_cap,), jnp.int32).at[slot_flat].set(remote_index.reshape(-1))
    )
    request = request.reshape(row_count, slot_cap)
    masked = remote_vals * remote_flag[:, :, None, None].astype(jnp.bfloat16)
    tiles_flat = masked.reshape(tile_count, block_size, block_size)
    piece = lax.all_to_all(request, "row", split_axis=0, concat_axis=0, tiled=True)
    found = xblocks[piece]
    returned = lax.all_to_all(found, "row", split_axis=0, concat_axis=0, tiled=True)
    remote_x = returned.reshape(row_count * slot_cap, block_size, feat)[slot_flat]
    remote_sum = jnp.einsum(
        "tij,tjf->tif", tiles_flat, remote_x, preferred_element_type=jnp.float32
    )
    remote_sum = jnp.sum(remote_sum.reshape(blocks_dev, tiles_row, block_size, feat), axis=1)
    local_x = xblocks[local_cols]
    local_sum = jnp.einsum(
        "rlij,rljf->rif", local_vals, local_x, preferred_element_type=jnp.float32
    )
    agg = (
        (xblocks.astype(jnp.float32) + local_sum + remote_sum)
        .reshape(node_count, feat)
        .astype(jnp.bfloat16)
    )
    degree = jnp.sum(local_vals, axis=(1, 3), dtype=jnp.float32) + jnp.sum(
        masked, axis=(1, 3), dtype=jnp.float32
    )
    norm = lax.rsqrt(1.0 + degree.reshape(node_count))
    z_value = norm[:, None] * jnp.dot(agg, weight, preferred_element_type=jnp.float32)
    activated, pull = jax.vjp(jax.nn.gelu, z_value)
    hidden = activated.astype(jnp.bfloat16)
    grad_z = pull(grad_out.astype(jnp.float32))[0]
    scaled_grad = (norm[:, None] * grad_z).astype(jnp.bfloat16)
    weight_term = lax.dot_general(
        agg, scaled_grad, (((0,), (0,)), ((), ())), preferred_element_type=jnp.float32
    )
    total_nodes = node_count * row_count
    weight_grad = lax.psum(weight_term, "row") * (1.0 / math.sqrt(total_nodes))
    dagg = lax.dot_general(
        scaled_grad, weight, (((1,), (1,)), ((), ())), preferred_element_type=jnp.float32
    ).astype(jnp.bfloat16)
    dblocks = dagg.reshape(blocks_dev, block_size, feat)
    local_hot = (
        local_cols[:, :, None] == jnp.arange(blocks_dev, dtype=jnp.int32)[None, None, :]
    ).astype(jnp.float32)
    local_terms = jnp.einsum(
        "rlij,rif->rljf", local_vals, dblocks, preferred_element_type=jnp.float32
    )
    local_back = jnp.einsum("rlk,rljf->kjf", local_hot, local_terms)
    asked_hot = (
        piece[:, :, None] == jnp.arange(blocks_dev, dtype=jnp.int32)[None, None, :]
    ).astype(jnp.bfloat16)
    sender_terms = jnp.einsum(
        "rtij,rif->rtjf", masked, dblocks, preferred_element_type=jnp.float32
    ).astype(jnp.bfloat16)
    part_send = (
        jnp.zeros((row_count * slot_cap, block_size, feat), jnp.bfloat16)
        .at[slot_flat]
        .set(sender_terms.reshape(tile_count, block_size, feat))
    )
    received = lax.all_to_all(
        part_send.reshape(row_count, slot_cap, block_size, feat),
        "row",
        split_axis=0,
        concat_axis=0,
        tiled=True,
    )
    remote_back = jnp.einsum(
        "sck,scjf->kjf", asked_hot, received, preferred_element_type=jnp.float32
    )
    input_grad = (
        (dblocks.astype(jnp.float32) + local_back + remote_back)
        .reshape(node_count, feat)
        .astype(jnp.bfloat16)
    )
    return (hidden, input_grad, weight_grad)


MESH = pl.DeviceIdType.MESH
RIGHT, LEFT, ACROSS, SIBLING = 0, 1, 2, 3
PIECES = 4


def place():
    me = lax.axis_index("row")
    core = lax.rem(me, 2)
    yy = lax.rem(lax.div(me, 2), 2)
    zz = lax.div(me, 4)
    return me, core, yy, zz, me + 1 - 2 * core, me + 2 - 4 * yy


def signal(barrier, device):
    pl.semaphore_signal(barrier, inc=1, device_id={"row": device}, device_id_type=MESH)


def split_rows(nodes):
    last = nodes // 8
    return (nodes - last) // PIECES, last


def gather_kernel(zs, x_ref, out_ref, own_sem, send_sem, recv_sem):
    me, core, yy, zz, sib, ynb = place()
    rows, tail = split_rows(x_ref.shape[0])
    has_left, has_right = zz > 0, zz < zs - 1

    barrier = pltpu.get_barrier_semaphore()
    signal(barrier, sib)
    signal(barrier, ynb)
    pl.when(has_left)(lambda: signal(barrier, me - 4))
    pl.when(has_right)(lambda: signal(barrier, me + 4))
    pl.semaphore_wait(barrier, 2 + has_left.astype(jnp.int32) + has_right.astype(jnp.int32))

    own = pltpu.make_async_copy(x_ref, out_ref.at[me], own_sem)
    own.start()

    def copy(kind, shard, j, device, mine=False):
        slot = lax.div(shard, 4) + zs * lax.rem(lax.div(shard, 2), 2)
        if j is None:
            cut, j = pl.ds(PIECES * rows, tail), PIECES
        else:
            cut = pl.ds(pl.multiple_of(j * rows, 16), rows)
        there = out_ref.at[shard, cut]
        return pltpu.make_async_remote_copy(
            src_ref=x_ref.at[cut] if mine else there,
            dst_ref=there,
            send_sem=send_sem.at[kind, slot, j],
            recv_sem=recv_sem.at[shard, j],
            device_id={"row": device},
            device_id_type=MESH,
        )

    def each(body):
        lax.fori_loop(0, PIECES, lambda j, c: (body(j), c)[1], 0)

    def valid(sign, k):
        return zz >= k if sign < 0 else zz + k < zs

    def own_sends(act):
        act(copy(ACROSS, me, None, ynb, True))

        def body(j):
            pl.when(has_right)(lambda: act(copy(RIGHT, me, j, me + 4, True)))
            pl.when(has_left)(lambda: act(copy(LEFT, me, j, me - 4, True)))
            act(copy(ACROSS, me, j, ynb, True))
            act(copy(SIBLING, me, j, sib, True))

        each(body)
        act(copy(SIBLING, me, None, sib, True))

    def tails_out(act, k):
        def go(kind, device):
            act(copy(kind, me, None, device, True))
            act(copy(kind, ynb, None, device))

        pl.when(jnp.logical_and(has_right, zz == k))(lambda: go(RIGHT, me + 4))
        pl.when(jnp.logical_and(has_left, zz == zs - 1 - k))(lambda: go(LEFT, me - 4))

    def along(act, wait):
        if wait:
            copy(SIBLING, ynb, None, sib).wait_recv()
        act(copy(SIBLING, ynb, None, sib))
        tails_out(act, 0)
        for k in range(1, zs):
            for sign in (-1, 1):
                shard = me + sign * 4 * k
                onward = has_right if sign < 0 else has_left
                kind = RIGHT if sign < 0 else LEFT

                def body(j, shard=shard, onward=onward, kind=kind, sign=sign):
                    if wait:
                        copy(SIBLING, shard, j, sib).wait_recv()
                    pl.when(onward)(lambda: act(copy(kind, shard, j, me - sign * 4)))
                    act(copy(ACROSS, shard, j, ynb))
                    act(copy(SIBLING, shard, j, sib))

                pl.when(valid(sign, k))(functools.partial(each, body))
            tails_out(act, k)
        for k in range(1, zs):
            for sign in (-1, 1):
                onward = has_right if sign < 0 else has_left
                kind = RIGHT if sign < 0 else LEFT

                @pl.when(valid(sign, k))
                def _(sign=sign, k=k, onward=onward, kind=kind):
                    for base in (me, ynb):
                        shard = base + sign * 4 * k
                        if wait:
                            copy(SIBLING, shard, None, sib).wait_recv()
                        pl.when(onward)(
                            lambda shard=shard: act(copy(kind, shard, None, me - sign * 4))
                        )
                        act(copy(SIBLING, shard, None, sib))

    def across(act, wait):
        for k in range(zs):
            for sign in (-1, 1):
                if k == 0 and sign == 1:
                    continue
                shard = ynb + sign * 4 * k

                def body(j, shard=shard):
                    if wait:
                        copy(SIBLING, shard, j, sib).wait_recv()
                    act(copy(SIBLING, shard, j, sib))

                pl.when(valid(sign, k))(functools.partial(each, body))

    start = lambda c: c.start()
    finish = lambda c: c.wait_send()
    own_sends(start)
    along(start, True)
    across(start, True)
    for q in range(2 * zs):
        shard = 2 * q + 1 - core
        each(lambda j, shard=shard: copy(SIBLING, shard, j, sib).wait_recv())
        copy(SIBLING, shard, None, sib).wait_recv()
    own.wait()
    own_sends(finish)
    along(finish, False)
    across(finish, False)


def gather(x, row_count):
    zs = row_count // 4
    return pl.pallas_call(
        functools.partial(gather_kernel, zs),
        out_shape=jax.ShapeDtypeStruct((row_count,) + x.shape, x.dtype),
        in_specs=[pl.BlockSpec(memory_space=pl.ANY)],
        out_specs=pl.BlockSpec(memory_space=pl.ANY),
        scratch_shapes=[
            pltpu.SemaphoreType.DMA,
            pltpu.SemaphoreType.DMA((4, 2 * zs, PIECES + 1)),
            pltpu.SemaphoreType.DMA((row_count, PIECES + 1)),
        ],
        compiler_params=pltpu.CompilerParams(
            collective_id=0, has_side_effects=True, vmem_limit_bytes=2 << 20
        ),
        cost_estimate=pl.CostEstimate(
            flops=1 << 35, bytes_accessed=64 * x.shape[0] * x.shape[1], transcendentals=0
        ),
        name="gather_features",
    )(x)


def layer_kernel(rows_step, lcol, owner, index, flag, x_ref, *refs):
    tiles_row = flag.shape[0]
    far = refs[: rows_step * tiles_row]
    refs = refs[rows_step * tiles_row :]
    weight_ref, grad_ref, lv_ref, rv_ref, hidden_ref, part_ref, base_ref, wg_ref = refs
    first = pl.program_id(0) * rows_step
    blocks_dev, block, feat = x_ref.shape
    lb = lv_ref.shape[1]
    f32, bf16 = jnp.float32, jnp.bfloat16

    @pl.when(first == 0)
    def _():
        base_ref[...] = jnp.zeros_like(base_ref)
        wg_ref[...] = jnp.zeros_like(wg_ref)

        def clear(i, c):
            at = pl.ds(pl.multiple_of(i * 8, 8), 8)
            part_ref[at] = jnp.zeros((8,) + part_ref.shape[1:], bf16)
            return c

        lax.fori_loop(0, part_ref.shape[0] // 8, clear, 0)

    ones = jnp.ones((block, feat), bf16)
    flags = [
        [flag[t, first + i].astype(f32) for t in range(tiles_row)] for i in range(rows_step)
    ]
    rows = [
        jnp.concatenate(
            [lv_ref[i, l] for l in range(lb)] + [rv_ref[i, t] for t in range(tiles_row)], axis=1
        )
        for i in range(rows_step)
    ]
    aggs, norms = [], []
    for i in range(rows_step):
        blocks = [
            jnp.concatenate([x_ref[lcol[l, first + i]], ones], axis=1) for l in range(lb)
        ]
        for t in range(tiles_row):
            seen = jnp.concatenate([far[i * tiles_row + t][0], ones], axis=1)
            blocks.append((seen.astype(f32) * flags[i][t]).astype(bf16))
        total = jnp.dot(rows[i], jnp.concatenate(blocks, axis=0), preferred_element_type=f32)
        aggs.append((x_ref[first + i].astype(f32) + total[:, :feat]).astype(bf16))
        norms.append(lax.rsqrt(1.0 + total[:, feat:]))
    agg = jnp.concatenate(aggs, axis=0)
    norm = jnp.concatenate(norms, axis=0)
    hid = weight_ref.shape[1]
    norm = jnp.concatenate([norm] * (hid // feat), axis=1)
    v = norm * jnp.dot(agg, weight_ref[...], preferred_element_type=f32)
    scale = math.sqrt(2.0 / math.pi)
    square = v * v
    t = jnp.tanh(scale * (v + 0.044715 * (square * v)))
    half = 0.5 * (1.0 + t)
    hidden_ref[...] = (v * half).astype(bf16)
    slope = half + (0.5 * scale) * v * (1.0 - t * t) * (1.0 + (3 * 0.044715) * square)
    gs = (norm * (grad_ref[...].astype(f32) * slope)).astype(bf16)
    dagg = lax.dot_general(
        weight_ref[...], gs, (((1,), (1,)), ((), ())), preferred_element_type=f32
    ).astype(bf16)
    wg_ref[...] += lax.dot_general(agg, gs, (((0,), (0,)), ((), ())), preferred_element_type=f32)
    for i in range(rows_step):
        down = dagg[:, i * block : (i + 1) * block]
        base_ref[first + i] += down.astype(f32)
        terms = jnp.dot(down, rows[i], preferred_element_type=f32)
        for l in range(lb):
            base_ref[lcol[l, first + i]] += terms[:, l * block : (l + 1) * block]
        for t in range(tiles_row):
            at = owner[t, first + i] * blocks_dev + index[t, first + i]
            term = terms[:, (lb + t) * block : (lb + t + 1) * block] * flags[i][t]
            part_ref[at] = (part_ref[at].astype(f32) + term).astype(bf16)


def layer(x, seen, weight, grad_out, local_vals, remote_vals, lcol, owner, index, flag):
    blocks_dev, lb, block, _ = local_vals.shape
    tiles_row = remote_vals.shape[1]
    feat, hid = weight.shape
    rows_step = 4
    whole = lambda *shape: pl.BlockSpec(shape, lambda r, *_: (0,) * len(shape))

    def seen_block(i, t):
        def at(r, lc, ow, ix, fl):
            row = r * rows_step + i
            return ow[t, row] * blocks_dev + ix[t, row], 0, 0

        return pl.BlockSpec((1, block, feat), at)

    far = [seen_block(i, t) for i in range(rows_step) for t in range(tiles_row)]
    return pl.pallas_call(
        functools.partial(layer_kernel, rows_step),
        grid_spec=pltpu.PrefetchScalarGridSpec(
            num_scalar_prefetch=4,
            grid=(blocks_dev // rows_step,),
            in_specs=[whole(blocks_dev, block, feat)]
            + far
            + [
                whole(feat, hid),
                pl.BlockSpec((rows_step * block, hid), lambda r, *_: (r, 0)),
                pl.BlockSpec((rows_step, lb, block, block), lambda r, *_: (r, 0, 0, 0)),
                pl.BlockSpec((rows_step, tiles_row, block, block), lambda r, *_: (r, 0, 0, 0)),
            ],
            out_specs=[
                pl.BlockSpec((rows_step * block, hid), lambda r, *_: (r, 0)),
                whole(seen.shape[0], feat, block),
                whole(blocks_dev, feat, block),
                whole(feat, hid),
            ],
        ),
        out_shape=[
            jax.ShapeDtypeStruct((blocks_dev * block, hid), jnp.bfloat16),
            jax.ShapeDtypeStruct((seen.shape[0], feat, block), jnp.bfloat16),
            jax.ShapeDtypeStruct((blocks_dev, feat, block), jnp.float32),
            jax.ShapeDtypeStruct((feat, hid), jnp.float32),
        ],
        compiler_params=pltpu.CompilerParams(
            dimension_semantics=("arbitrary",), vmem_limit_bytes=28 << 20
        ),
        name="layer",
    )(
        lcol,
        owner,
        index,
        flag,
        x,
        *([seen] * (rows_step * tiles_row)),
        weight,
        grad_out,
        local_vals,
        remote_vals,
    )


def scatter_kernel(
    zs,
    part_ref,
    base_ref,
    w_ref,
    out_ref,
    wout_ref,
    mine,
    from_core,
    from_y,
    from_z,
    tail_z,
    held,
    base_sum,
    w_in,
    w_sum,
    load_sem,
    send_sem,
    core_sem,
    y_sem,
    z_sem,
    tail_send,
    tail_sem,
    w_send,
    w_recv,
):
    me, core, yy, zz, sib, ynb = place()
    rows, tail = split_rows(part_ref.shape[1])
    has_left, has_right = zz > 0, zz < zs - 1
    f32, bf16 = jnp.float32, jnp.bfloat16
    near = me + 4 * (1 - 2 * lax.rem(zz, 2))
    apart = me + 8 * (1 - 2 * lax.div(zz, 2))

    def load(zt, yt):
        q = yt * zs + zt
        return pltpu.make_async_copy(
            part_ref.at[zt * 4 + yt * 2 + core], mine.at[q], load_sem.at[q]
        )

    for yt in range(2):
        for zt in range(zs):
            load(zt, yt).start()

    barrier = pltpu.get_barrier_semaphore()
    signal(barrier, sib)
    signal(barrier, ynb)
    signal(barrier, apart)
    pl.when(has_left)(lambda: signal(barrier, me - 4))
    pl.when(has_right)(lambda: signal(barrier, me + 4))
    pl.semaphore_wait(barrier, 3 + has_left.astype(jnp.int32) + has_right.astype(jnp.int32))

    def each(body):
        lax.fori_loop(0, PIECES, lambda j, c: (body(j), c)[1], 0)

    def cut(j):
        if isinstance(j, int):
            return pl.ds(PIECES * rows, tail)
        return pl.ds(pl.multiple_of(j * rows, 16), rows)

    def remote(src, dst, send, recv, device):
        return pltpu.make_async_remote_copy(
            src_ref=src,
            dst_ref=dst,
            send_sem=send,
            recv_sem=recv,
            device_id={"row": device},
            device_id_type=MESH,
        )

    wrows = w_ref.shape[0] // 2
    kept = pl.ds(pl.multiple_of(core * wrows, wrows), wrows)
    given = pl.ds(pl.multiple_of((1 - core) * wrows, wrows), wrows)
    w_steps = [
        remote(w_ref.at[given], w_in.at[0], w_send.at[0], w_recv.at[0], sib),
        remote(w_sum.at[0], w_in.at[1], w_send.at[1], w_recv.at[1], ynb),
        remote(w_sum.at[1], w_in.at[2], w_send.at[2], w_recv.at[2], near),
        remote(w_sum.at[2], w_in.at[3], w_send.at[3], w_recv.at[3], apart),
    ]
    w_last = remote(wout_ref.at[kept], wout_ref.at[kept], w_send.at[4], w_recv.at[4], sib)
    w_back = remote(wout_ref.at[given], wout_ref.at[given], w_send.at[4], w_recv.at[4], sib)

    def w_go(step):
        w_steps[step].wait_recv()
        held_so_far = w_ref[kept] if step == 0 else w_sum[step - 1]
        total = held_so_far + w_in[step]
        if step < 3:
            w_sum[step] = total
            w_steps[step + 1].start()
        else:
            wout_ref[kept] = total
            w_last.start()

    w_steps[0].start()

    def valid(sign, d):
        return zz >= d if sign < 0 else zz + d < zs

    def order(least):
        for d in range(zs - 1, least - 1, -1):
            for sign in (1, -1) if d else (1,):
                yield d, sign

    def to_core(zt, yt, j):
        return remote(
            part_ref.at[zt * 4 + yt * 2 + 1 - core, cut(j)],
            from_core.at[yt * zs + zt, cut(j)],
            send_sem.at[yt * zs + zt, j],
            core_sem.at[yt * zs + zt, j],
            sib,
        )

    def to_y(zt, j):
        return remote(
            held.at[(1 - yy) * zs + zt, cut(j)],
            from_y.at[zt, cut(j)],
            send_sem.at[2 * zs + zt, j],
            y_sem.at[zt, j],
            ynb,
        )

    def to_z(zt, way, j, device):
        return remote(
            held.at[yy * zs + zt, cut(j)],
            from_z.at[way, zt, cut(j)],
            send_sem.at[3 * zs + zt, j],
            z_sem.at[way, zt, j],
            device,
        )

    def to_next(zt, yt, way, device):
        q = yt * zs + zt
        return remote(
            held.at[q, cut(PIECES)],
            tail_z.at[way, q],
            tail_send.at[q],
            tail_sem.at[way, q],
            device,
        )

    def tail_sum(zt, yt):
        q = yt * zs + zt
        to_core(zt, yt, PIECES).wait_recv()
        return mine[q, cut(PIECES)].astype(f32) + from_core[q, cut(PIECES)].astype(f32)

    def core_sends(yt, d, sign):
        zt = zz + sign * d
        pl.when(valid(sign, d))(functools.partial(each, lambda j: to_core(zt, yt, j).start()))

    near_first = list(order(0))
    for d, sign in near_first[:2]:
        core_sends(1 - yy, d, sign)
    for d, sign in near_first:
        zt = zz + sign * d

        @pl.when(valid(sign, d))
        def _(zt=zt):
            to_core(zt, 1 - yy, PIECES).start()
            to_core(zt, yy, PIECES).start()

    for d, sign in near_first[2:]:
        core_sends(1 - yy, d, sign)
    for d, sign in near_first:
        core_sends(yy, d, sign)

    w_go(0)
    for yt in range(2):
        for zt in range(zs):
            load(zt, yt).wait()

    for d in range(zs - 1, -1, -1):
        for sign in (1, -1) if d else (1,):
            zt = zz + sign * d

            @pl.when(valid(sign, d))
            def _(zt=zt):
                q = (1 - yy) * zs + zt

                def body(j):
                    to_core(zt, 1 - yy, j).wait_recv()
                    total = mine[q, cut(j)].astype(f32) + from_core[q, cut(j)].astype(f32)
                    held[q, cut(j)] = total.astype(bf16)
                    to_y(zt, j).start()

                each(body)

        for sign in (1, -1) if d else ():
            zt = zz + sign * d
            way = 0 if sign > 0 else 1
            behind = has_left if sign > 0 else has_right

            @pl.when(valid(sign, d))
            def _(zt=zt, way=way, behind=behind, sign=sign):
                for yt in (1 - yy, yy):
                    q = yt * zs + zt
                    total = tail_sum(zt, yt)

                    @pl.when(behind)
                    def _():
                        to_next(zt, yt, way, sib).wait_recv()
                        held[q, cut(PIECES)] = (total + tail_z[way, q].astype(f32)).astype(bf16)

                    @pl.when(jnp.logical_not(behind))
                    def _():
                        held[q, cut(PIECES)] = total.astype(bf16)

                    to_next(zt, yt, way, me + sign * 4).start()

    for yt in (1 - yy, yy):
        q = yt * zs + zz
        base_sum[cut(PIECES)] = tail_sum(zz, yt)
        for way, behind in ((0, has_left), (1, has_right)):

            @pl.when(behind)
            def _(way=way, q=q, yt=yt):
                to_next(zz, yt, way, sib).wait_recv()
                base_sum[cut(PIECES)] += tail_z[way, q].astype(f32)

        if yt is not yy:
            held[q, cut(PIECES)] = base_sum[cut(PIECES)].astype(bf16)
            to_y(zz, PIECES).start()

    def summed(zt, j):
        q = yy * zs + zt
        to_core(zt, yy, j).wait_recv()
        to_y(zt, j).wait_recv()
        total = mine[q, cut(j)].astype(f32) + from_core[q, cut(j)].astype(f32)
        return total + from_y[zt, cut(j)].astype(f32)

    w_go(1)
    step = 2
    for d, sign in order(1):
        zt = zz + sign * d
        way = 0 if sign > 0 else 1
        behind = has_left if sign > 0 else has_right

        @pl.when(valid(sign, d))
        def _(zt=zt, way=way, behind=behind, sign=sign):

            def body(j):
                total = summed(zt, j)
                q = yy * zs + zt

                @pl.when(behind)
                def _():
                    to_z(zt, way, j, me + sign * 4).wait_recv()
                    held[q, cut(j)] = (total + from_z[way, zt, cut(j)].astype(f32)).astype(bf16)

                @pl.when(jnp.logical_not(behind))
                def _():
                    held[q, cut(j)] = total.astype(bf16)

                to_z(zt, way, j, me + sign * 4).start()

            each(body)

        if sign < 0 and step < 4:
            w_go(step)
            step += 1

    def last(j):
        base_sum[cut(j)] = base_ref[cut(j)] + summed(zz, j)

        @pl.when(has_left)
        def _():
            to_z(zz, 0, j, sib).wait_recv()
            base_sum[cut(j)] += from_z[0, zz, cut(j)].astype(f32)

        @pl.when(has_right)
        def _():
            to_z(zz, 1, j, sib).wait_recv()
            base_sum[cut(j)] += from_z[1, zz, cut(j)].astype(f32)

        out_ref[cut(j)] = base_sum[cut(j)].astype(bf16)

    each(last)
    to_y(zz, PIECES).wait_recv()
    total = base_ref[cut(PIECES)] + base_sum[cut(PIECES)]
    out_ref[cut(PIECES)] = (total + from_y[zz, cut(PIECES)].astype(f32)).astype(bf16)

    w_back.wait_recv()
    for c in w_steps:
        c.wait_send()
    w_last.wait_send()
    to_y(zz, PIECES).wait_send()
    for zt in range(zs):
        for yt in range(2):
            to_core(zt, yt, PIECES).wait_send()
            pl.when(zz != zt)(lambda zt=zt, yt=yt: to_next(zt, yt, 0, sib).wait_send())
        each(lambda j, zt=zt: to_core(zt, 0, j).wait_send())
        each(lambda j, zt=zt: to_core(zt, 1, j).wait_send())
        each(lambda j, zt=zt: to_y(zt, j).wait_send())
        pl.when(zz != zt)(
            functools.partial(each, lambda j, zt=zt: to_z(zt, 0, j, sib).wait_send())
        )


def scatter(part, base, wterm, row_count):
    zs = row_count // 4
    nodes, feat = base.shape
    vmem = pl.BlockSpec(memory_space=pltpu.VMEM)
    dma = pltpu.SemaphoreType.DMA
    shard = lambda *lead: pltpu.VMEM(lead + (nodes, feat), jnp.bfloat16)
    wshape = (wterm.shape[0] // 2, wterm.shape[1])
    return pl.pallas_call(
        functools.partial(scatter_kernel, zs),
        out_shape=[
            jax.ShapeDtypeStruct((nodes, feat), jnp.bfloat16),
            jax.ShapeDtypeStruct(wterm.shape, jnp.float32),
        ],
        in_specs=[pl.BlockSpec(memory_space=pl.ANY), vmem, vmem],
        out_specs=[vmem, vmem],
        scratch_shapes=[
            shard(2 * zs),
            shard(2 * zs),
            shard(zs),
            shard(2, zs),
            pltpu.VMEM((2, 2 * zs, split_rows(nodes)[1], feat), jnp.bfloat16),
            shard(2 * zs),
            pltpu.VMEM((nodes, feat), jnp.float32),
            pltpu.VMEM((4,) + wshape, jnp.float32),
            pltpu.VMEM((3,) + wshape, jnp.float32),
            dma((2 * zs,)),
            dma((4 * zs, PIECES + 1)),
            dma((2 * zs, PIECES + 1)),
            dma((zs, PIECES + 1)),
            dma((2, zs, PIECES)),
            dma((2 * zs,)),
            dma((2, 2 * zs)),
            dma((5,)),
            dma((5,)),
        ],
        compiler_params=pltpu.CompilerParams(
            collective_id=1, has_side_effects=True, vmem_limit_bytes=24 << 20
        ),
        name="scatter_gradient",
    )(part, base, wterm)


def planned(
    features,
    weight,
    grad_out,
    local_vals,
    local_cols,
    remote_vals,
    remote_owner,
    remote_index,
    remote_flag,
):
    blocks_dev, _, block, _ = local_vals.shape
    nodes, feat = features.shape
    row_count = lax.axis_size("row")
    seen = gather(features, row_count).reshape(row_count * blocks_dev, block, feat)
    hidden, part, base, wterm = layer(
        features.reshape(blocks_dev, block, feat),
        seen,
        weight,
        grad_out,
        local_vals,
        remote_vals,
        local_cols.T,
        remote_owner.T,
        remote_index.T,
        remote_flag.T,
    )
    back, wsum = scatter(
        part.reshape(row_count, nodes, feat), base.reshape(nodes, feat), wterm, row_count
    )
    input_grad = jnp.swapaxes(back.reshape(blocks_dev, feat, block), 1, 2).reshape(nodes, feat)
    weight_grad = wsum * (1.0 / math.sqrt(nodes * row_count))
    return hidden, input_grad, weight_grad


def solution(mesh):
    return jax.shard_map(
        planned if mesh.shape["row"] == 16 else slotted,
        mesh=mesh,
        in_specs=(
            P(("grp", "row"), None),
            P(),
            P(("grp", "row"), None),
            P(("grp", "row"), None, None, None),
            P(("grp", "row"), None),
            P(("grp", "row"), None, None, None),
            P(("grp", "row"), None),
            P(("grp", "row"), None),
            P(("grp", "row"), None),
        ),
        out_specs=(P(("grp", "row"), None), P(("grp", "row"), None), P("grp", None)),
        check_vma=False,
    )
```
